256 devices in a mesh: row: 4 (over x), col: 8 (over y, core), layer: 8 (over z).
Axes of the slice: x: 4, y: 4, z: 8, core: 2. Of those that a mesh axis runs over, the one named last changes fastest.
Arguments:
- blocks: float32 [128, 16, 128, 128], P(('row', 'col'), 'layer'), as said below
- columns: int32 [128, 16], replicated, may hold values from -1 to 127, as said below
- signs: int32 [3], replicated, may hold values from 0 to 1, as said below
Outputs:
- purified: float32 [128, 16, 128, 128], P(('row', 'col'), 'layer')
- traces: float32 [3], replicated
The draws below stay inside these ranges and needn't reach their ends.
Inputs may be any that keep to these rules, and one draw needn't show every extreme that they name: Slots l * 2 to (l + 1) * 2 - 1 of row i hold, in increasing order and then padded with -1, the block columns j of row i's pattern with j % 8 = l. Every j satisfies |i - j| <= 4. The pattern is symmetric and holds every j with |i - j| <= 1 or |i - j| = 4. blocks[i, q] is the block (i, columns[i, q]) of a symmetric matrix: block (j, i) is the transpose of block (i, j). Empty slots hold zeros. `signs`: both branches occur among the 3 steps.
All inputs are finite; a program needn't handle non-finite values.
Results may differ from the reference program's by a relative error of at most 0.0003.
Values sent between devices are 32-bit elements; how exact they have to be, the bound alone decides.
A program may use at most 128 MiB of HBM per device.

```python
import jax
import jax.numpy as jnp
import numpy as np
from jax import lax

BLOCK = 128
NEAR = 4
ITERS = 3
NB = 128
SLOT = 2
ROW_SLOTS = 16
N_LAYER = 8


def pattern_table(key):
    row_ids = jnp.arange(NB, dtype=jnp.int32)[:, None]
    offsets = jnp.arange(-NEAR, NEAR + 1, dtype=jnp.int32)[None, :] + 0 * row_ids
    targets = row_ids + offsets
    inside = (targets >= 0) & (targets < NB)
    lower_row = jnp.clip(jnp.minimum(row_ids, targets), 0, NB - 1)
    distance = jnp.abs(offsets)
    density = 40 + 60 * lower_row // NB
    rolls = jax.random.randint(jax.random.fold_in(key, 101), (NB, NEAR + 1), 0, 100)
    picked = rolls[lower_row, distance]
    keep_pair = inside & ((distance <= 1) | (distance == NEAR) | (picked < density))
    span_ids = np.arange(2 * NEAR + 1)
    earlier = (span_ids[None, :] < span_ids[:, None]) & ((span_ids[:, None] - span_ids[None, :]) % N_LAYER == 0)
    rank = jnp.sum(keep_pair[:, None, :].astype(jnp.int32) * jnp.asarray(earlier, jnp.int32)[None], axis=2)
    residue = jnp.mod(targets, N_LAYER)
    slot_ids = residue * SLOT + rank
    return (keep_pair, targets, slot_ids, lower_row, distance, offsets)


def draw_columns(key, part):
    keep_pair, targets, slot_ids, lower_row, distance, offsets = pattern_table(key)
    hits = (slot_ids[:, :, None] == jnp.arange(ROW_SLOTS, dtype=jnp.int32)[None, None, :]) & keep_pair[:, :, None]
    return (jnp.sum(jnp.where(hits, targets[:, :, None] + 1, 0), axis=1) - 1).astype(jnp.int32)


def draw_signs(key, part):
    key = jax.random.fold_in(key, 7)
    code = jax.random.randint(key, (), 1, 2 ** ITERS - 1)
    powers = 2 ** jnp.arange(ITERS, dtype=jnp.int32)
    return (code // powers % 2).astype(jnp.int32)


def draw_blocks(key, part):
    keep_pair, targets, slot_ids, lower_row, distance, offsets = pattern_table(key)
    key = jax.random.fold_in(key, 5)
    row_frac = jnp.arange(NB, dtype=jnp.float32)[:, None] / NB
    pairs = jax.random.normal(jax.random.fold_in(key, 1), (NB, NEAR + 1, BLOCK, BLOCK), jnp.float32) * 0.006
    onsite = jax.random.uniform(jax.random.fold_in(key, 2), (NB, BLOCK), jnp.float32, 0.1, 1.0) * (0.3 + 0.6 * row_frac)
    values = pairs[lower_row, distance]
    flipped = jnp.swapaxes(values, 2, 3)
    values = jnp.where((offsets < 0)[:, :, None, None], flipped, values)
    diagonal = (values + flipped) * 0.7071 + onsite[:, None, :, None] * jnp.eye(BLOCK, dtype=jnp.float32)
    values = jnp.where((offsets == 0)[:, :, None, None], diagonal, values)
    slot_safe = jnp.where(keep_pair, slot_ids, ROW_SLOTS)
    row_index = jnp.broadcast_to(jnp.arange(NB, dtype=jnp.int32)[:, None], slot_safe.shape)
    spread = jnp.zeros((NB, ROW_SLOTS + 1, BLOCK, BLOCK), jnp.float32).at[row_index, slot_safe].set(values)
    return spread[:, :ROW_SLOTS]


def setup_inputs(seed: int = 0) -> dict:
    keys = jax.random.split(jax.random.key(seed), 4)
    blocks = draw_blocks(jax.random.fold_in(keys[3], 71), 0)
    columns = draw_columns(jax.random.fold_in(keys[3], 71), 0)
    signs = draw_signs(jax.random.fold_in(keys[3], 71), 0)
    return dict(blocks=blocks, columns=columns, signs=signs)


def square_rows(current, columns):
    slot_count = current.shape[1]

    def one_row(index):
        own_blocks = current[index]
        own_slots = columns[index]
        locate = jnp.maximum(own_slots, 0)
        their_cols = columns[locate]
        matches = (own_slots[None, :, None] == their_cols[:, None, :]) & (own_slots[None, :, None] >= 0)
        position = jnp.sum(matches * jnp.arange(slot_count, dtype=jnp.int32)[None, None, :], axis=2).astype(jnp.int32)
        present = jnp.any(matches, axis=2)
        partner = current[locate[:, None], position]
        partner = jnp.where(present[:, :, None, None], partner, jnp.float32(0.0))
        result = jnp.einsum("sac,qsbc->qab", own_blocks, partner, precision=lax.Precision.HIGHEST)
        return jnp.where((own_slots >= 0)[:, None, None], result, jnp.float32(0.0))

    return lax.map(one_row, jnp.arange(current.shape[0], dtype=jnp.int32))


def reference(blocks, columns, signs):
    current = blocks
    row_ids = jnp.arange(blocks.shape[0], dtype=jnp.int32)[:, None]
    is_diag = columns == row_ids
    results = []
    for iteration in range(ITERS):
        squared = square_rows(current, columns)
        current = jnp.where(signs[iteration] == 1, squared, 2.0 * current - squared)
        diag_trace = jnp.sum(jnp.where(is_diag, jnp.trace(current, axis1=2, axis2=3), jnp.float32(0.0)))
        results.append(diag_trace)
    traces = jnp.stack(results) / (NB * BLOCK)
    return current, traces
```

```python
import jax
import jax.numpy as jnp
from jax import lax
from jax.experimental import pallas as pl
from jax.experimental.pallas import tpu as pltpu
from jax.sharding import PartitionSpec as P

MESH = pl.DeviceIdType.MESH
B = 128
H = 4
D = 5
STEPS = 3
LEFT_TILES = ((0, 0, (4, 10), (0, 4)), (0, 1, (4, 10), (2, 4)), (1, 1, (4, 12), (2, 4)))
RIGHT_TILES = ((0, 2, (4, 8), (8, 10)), (1, 2, (4, 8), (8, 12)), (1, 3, (6, 8), (8, 12)))
TILES = LEFT_TILES + RIGHT_TILES
UPPER = tuple((a, d) for a in range(H) for d in range(D))
INNER = tuple((a, d) for a, d in UPPER if a + d < H)
OUTER = tuple((a, d) for a, d in UPPER if a + d >= H)


def at_layer(group):
    return 4 * lax.rem(group // 2 + group, 2)


def kernel(groups, n_col, n_layer, cols_ref, signs_ref, blk_ref, out_ref, tr_ref, own, left, right, high, low, acc, flip,
           zero, tb1, tb2, tb3, gsend, grecv, hsend, hrecv, osend, orecv, zsem, t1s, t1r, t2s, t2r, t3s, t3r):
    row, col, layer = lax.axis_index("row"), lax.axis_index("col"), lax.axis_index("layer")
    n_row = groups // n_col
    g = row * n_col + col
    after, before = lax.rem(g + 1, groups), lax.rem(g + groups - 1, groups)
    zc = at_layer(g)
    collector = layer == zc
    base = lax.rem(H * g, n_layer)
    u = lax.rem(layer - base + n_layer, n_layer)

    def place(group, at):
        return (group // n_col, lax.rem(group, n_col), at)

    def head(group):
        return place(group, at_layer(group))

    def slot_up(group):
        return jnp.where(group == 0, 0, 1)

    def remote(src, dst, send, recv, to):
        return pltpu.make_async_remote_copy(src, dst, send, recv, device_id=to, device_id_type=MESH)

    def arrived(ref, sem):
        pltpu.make_async_copy(ref, ref, sem).wait()

    barrier = pltpu.get_barrier_semaphore()

    def greet(to):
        pl.semaphore_signal(barrier, inc=1, device_id=to, device_id_type=MESH)

    greet(head(before))

    @pl.when(jnp.logical_not(collector))
    def _():
        greet(head(g))
        pl.semaphore_wait(barrier, 1)

    @pl.when(collector)
    def _():
        greet(head(after))
        for p in range(1, n_layer):
            greet(place(g, lax.rem(layer + p, n_layer)))
        for p in range(1, n_col):
            greet(head(row * n_col + lax.rem(col + p, n_col)))
        for p in range(1, n_row):
            greet(head(lax.rem(row + p, n_row) * n_col + col))
        pl.semaphore_wait(barrier, (n_layer - 1) + n_layer + 1 + (n_col - 1) + (n_row - 1))

    def source(a):
        d = u - a
        return d, jnp.where(d == D - 1, slot_up(g), 0)

    for a in range(H):
        d, slot = source(a)
        has = (d >= 0) & (d < D)

        @pl.when(has & jnp.logical_not(collector))
        def _():
            remote(blk_ref.at[a, slot], own.at[0, a, d], gsend.at[a], grecv.at[a, d], head(g)).start()

        @pl.when(has & collector)
        def _():
            pltpu.make_async_copy(blk_ref.at[a, slot], own.at[0, a, d], grecv.at[a, d]).start()

    zero[...] = jnp.zeros_like(zero)
    for a in range(H):
        @pl.when(u != a + H)
        def _():
            pltpu.make_async_copy(zero, out_ref.at[a, 1], zsem.at[a]).start()

    def to_before(t, a):
        part = pl.ds(0, H - a)
        return remote(own.at[t, a, part], right.at[t, a, part], hsend.at[t, 0, a], hrecv.at[t, 0, a], head(before))

    def to_after(t, a):
        part = pl.ds(H - a, a + 1)
        return remote(own.at[t, a, part], left.at[t, a, part], hsend.at[t, 1, a], hrecv.at[t, 1, a], head(after))

    def put(r, k, x):
        h = x.astype(jnp.bfloat16)
        high[r * B:(r + 1) * B, k * B:(k + 1) * B] = h
        low[r * B:(r + 1) * B, k * B:(k + 1) * B] = (x - h.astype(jnp.float32)).astype(jnp.bfloat16)

    def product(i, j, span):
        def part(ref, r):
            return ref[2 * B * r:2 * B * (r + 1), span[0] * B:span[1] * B]

        def dot(x, y):
            return lax.dot_general(x, y, (((1,), (1,)), ((), ())), preferred_element_type=jnp.float32)

        ah, al, bh, bl = part(high, i), part(low, i), part(high, j), part(low, j)
        return dot(ah, bh) + (dot(al, bh) + dot(ah, bl))

    def finish(t, tiles):
        square = signs_ref[t] == 1
        keep = jnp.where(square, 0.0, 2.0).astype(jnp.float32)
        sign = jnp.where(square, 1.0, -1.0).astype(jnp.float32)
        for i, j, inner, outer in tiles:
            n = TILES.index((i, j, inner, outer))
            tile = acc[n] + product(i, j, outer)
            for a in (2 * i, 2 * i + 1):
                for q in (2 * j, 2 * j + 1):
                    d = q - a
                    if 0 <= d < D:
                        at_row = H * g + a
                        at_col = at_row + d
                        slot = 2 * lax.rem(at_col, n_layer)
                        there = (cols_ref[at_row, slot] == at_col) | (cols_ref[at_row, slot + 1] == at_col)
                        factor = jnp.where(there, sign, 0.0)
                        part = tile[(a % 2) * B:(a % 2 + 1) * B, (q % 2) * B:(q % 2 + 1) * B]
                        own[t + 1, a, d] = keep * own[t, a, d] + factor * part

    def share_traces():
        eye = lax.broadcasted_iota(jnp.int32, (B, B), 0) == lax.broadcasted_iota(jnp.int32, (B, B), 1)

        def diagonal(t):
            total = own[t, 0, 0]
            for a in range(1, H):
                total = total + own[t, a, 0]
            return jnp.sum(jnp.where(eye, total, 0.0), axis=0, keepdims=True)

        one, two = diagonal(1), diagonal(2)
        diag = jnp.zeros((B, B), jnp.float32)
        off = jnp.zeros((B, B), jnp.float32)
        for a, d in UPPER:
            x = own[2, a, d]
            if d:
                off = off + x * x
            else:
                diag = diag + x * x
        norm = jnp.sum(diag + 2.0 * off, axis=0, keepdims=True)
        three = jnp.where(signs_ref[2] == 1, norm, 2.0 * two - norm)
        line = lax.broadcasted_iota(jnp.int32, (8, B), 0)
        tb1[col] = jnp.where(line == 0, one, jnp.where(line == 1, two, jnp.where(line == 2, three, 0.0)))
        for p in range(1, n_col):
            to = head(row * n_col + lax.rem(col + p, n_col))
            remote(tb1.at[col], tb1.at[col], t1s.at[p], t1r.at[col], to).start()

    def share_rows():
        for p in range(1, n_col):
            c = lax.rem(col + p, n_col)
            arrived(tb1.at[c], t1r.at[c])
        tb2[row] = jnp.sum(tb1[...], axis=0)
        for p in range(1, n_row):
            to = head(lax.rem(row + p, n_row) * n_col + col)
            remote(tb2.at[row], tb2.at[row], t2s.at[p], t2r.at[row], to).start()

    def share_layers():
        for p in range(1, n_row):
            r = lax.rem(row + p, n_row)
            arrived(tb2.at[r], t2r.at[r])
        total = jnp.sum(jnp.sum(tb2[...], axis=0), axis=1, keepdims=True) / (groups * H * B)
        tb3[...] = jnp.broadcast_to(total, (8, B))
        for p in range(1, n_layer):
            remote(tb3, tb3, t3s.at[p], t3r, place(g, lax.rem(layer + p, n_layer))).start()

    @pl.when(collector)
    def _():
        high[...] = jnp.zeros_like(high)
        low[...] = jnp.zeros_like(low)
        for a in range(H):
            for d in range(H - a):
                arrived(own.at[0, a, d], grecv.at[a, d])
            to_before(0, a).start()
        for a in range(H):
            for d in range(H - a, D):
                arrived(own.at[0, a, d], grecv.at[a, d])
            to_after(0, a).start()

        def step(t, carry):
            for a, d in UPPER:
                x = own[t, a, d]
                put(a, H + a + d, x)
                if d:
                    put(a + d, H + a, x.T)
            pl.when(t == 2)(share_traces)
            for n, (i, j, inner, _) in enumerate(TILES):
                acc[n] = product(i, j, inner)
            pl.when(t == 2)(share_rows)
            for a in range(H):
                part = pl.ds(H - a, a + 1)
                arrived(left.at[t, a, part], hrecv.at[t, 1, a])
            for a, d in OUTER:
                put(a + d - H, a, left[t, a, d].T)
            finish(t, LEFT_TILES)

            @pl.when(t < 2)
            def _():
                for a in range(H):
                    to_before(t + 1, a).start()

            for a in range(H):
                part = pl.ds(0, H - a)
                arrived(right.at[t, a, part], hrecv.at[t, 0, a])
            for a, d in INNER:
                x = right[t, a, d]
                put(H + a, 2 * H + a + d, x)
                if d:
                    put(H + a + d, 2 * H + a, x.T)
            finish(t, RIGHT_TILES)

            @pl.when(t < 2)
            def _():
                for a in range(H):
                    to_after(t + 1, a).start()

            pl.when(t == 2)(share_layers)
            return carry

        lax.fori_loop(0, STEPS, step, 0)

        for a, d in UPPER:
            if d:
                flip[a, d] = own[STEPS, a, d].T

        for done in (False, True):
            for a, d in UPPER:
                q = a + d
                way = [(0, own.at[STEPS, a, d], g, lax.rem(base + q, n_layer), a, slot_up(g) if d == H else 0)]
                if d:
                    src = flip.at[a, d]
                    if q < H:
                        way.append((1, src, g, lax.rem(base + a, n_layer), q, 0))
                    else:
                        slot = 1 - slot_up(after) if d == H else 0
                        way.append((1, src, after, lax.rem(base + a, n_layer), q - H, slot))
                for n, src, group, at, r, slot in way:
                    sem = osend.at[n, a, d]
                    far = remote(src, out_ref.at[r, slot], sem, orecv.at[r, slot], place(group, at))
                    if n == 1 and q >= H:
                        far.wait_send() if done else far.start()
                        continue
                    here = at == layer

                    @pl.when(jnp.logical_not(here))
                    def _():
                        far.wait_send() if done else far.start()

                    if not done:
                        @pl.when(here)
                        def _():
                            pltpu.make_async_copy(src, out_ref.at[r, slot], orecv.at[r, slot]).start()

        for t in range(STEPS):
            for a in range(H):
                to_before(t, a).wait_send()
                to_after(t, a).wait_send()
        for p in range(1, n_col):
            remote(tb1.at[col], tb1.at[col], t1s.at[p], t1r.at[col], head(g)).wait_send()
        for p in range(1, n_row):
            remote(tb2.at[row], tb2.at[row], t2s.at[p], t2r.at[row], head(g)).wait_send()
        for p in range(1, n_layer):
            remote(tb3, tb3, t3s.at[p], t3r, head(g)).wait_send()

    @pl.when(jnp.logical_not(collector))
    def _():
        for a in range(H):
            d, slot = source(a)

            @pl.when((d >= 0) & (d < D))
            def _():
                remote(blk_ref.at[a, slot], own.at[0, a, d], gsend.at[a], grecv.at[a, d], head(g)).wait_send()

        arrived(tb3, t3r)

    for t in range(STEPS):
        tr_ref[t] = tb3[t, 0]
    for a in range(H):
        arrived(out_ref.at[a, 0], orecv.at[a, 0])

        @pl.when(u == a + H)
        def _():
            arrived(out_ref.at[a, 1], orecv.at[a, 1])

        @pl.when(u != a + H)
        def _():
            pltpu.make_async_copy(zero, out_ref.at[a, 1], zsem.at[a]).wait()


def solution(mesh):
    n_row, n_col, n_layer = (mesh.shape[name] for name in ("row", "col", "layer"))
    groups = n_row * n_col
    dma = pltpu.SemaphoreType.DMA

    def shards(blocks, columns, signs):
        def body(*refs):
            kernel(groups, n_col, n_layer, *refs)

        f32, bf16 = jnp.float32, jnp.bfloat16
        return pl.pallas_call(
            body,
            out_shape=(jax.ShapeDtypeStruct(blocks.shape, f32), jax.ShapeDtypeStruct((STEPS,), f32)),
            in_specs=[
                pl.BlockSpec(memory_space=pltpu.SMEM),
                pl.BlockSpec(memory_space=pltpu.SMEM),
                pl.BlockSpec(memory_space=pl.ANY),
            ],
            out_specs=(pl.BlockSpec(memory_space=pl.ANY), pl.BlockSpec(memory_space=pltpu.SMEM)),
            scratch_shapes=[
                pltpu.VMEM((STEPS + 1, H, D, B, B), f32),
                pltpu.VMEM((STEPS, H, D, B, B), f32),
                pltpu.VMEM((STEPS, H, D, B, B), f32),
                pltpu.VMEM((2 * H * B, 3 * H * B), bf16),
                pltpu.VMEM((2 * H * B, 3 * H * B), bf16),
                pltpu.VMEM((len(TILES), 2 * B, 2 * B), f32),
                pltpu.VMEM((H, D, B, B), f32),
                pltpu.VMEM((B, B), f32),
                pltpu.VMEM((n_col, 8, B), f32),
                pltpu.VMEM((n_row, 8, B), f32),
                pltpu.VMEM((8, B), f32),
                dma((H,)),
                dma((H, D)),
                dma((STEPS, 2, H)),
                dma((STEPS, 2, H)),
                dma((2, H, D)),
                dma((H, 2)),
                dma((H,)),
                dma((n_col,)),
                dma((n_col,)),
                dma((n_row,)),
                dma((n_row,)),
                dma((n_layer,)),
                dma,
            ],
            compiler_params=pltpu.CompilerParams(
                collective_id=0, has_side_effects=True, vmem_limit_bytes=48 * 1024 * 1024
            ),
        )(columns, signs, blocks)

    return jax.shard_map(
        shards,
        mesh=mesh,
        in_specs=(P(("row", "col"), "layer", None, None), P(), P()),
        out_specs=(P(("row", "col"), "layer", None, None), P()),
        check_vma=False,
    )
```

```python
import jax
import jax.numpy as jnp
from jax import lax
from jax.experimental import pallas as pl
from jax.experimental.pallas import tpu as pltpu
from jax.sharding import PartitionSpec as P

MESH = pl.DeviceIdType.MESH
B = 128
ROWS = 4
STEPS = 3
BLOCKS = ((0, 0), (0, 1), (1, 1), (0, 2), (0, 3), (1, 2), (1, 3), (0, 4), (1, 4), (1, 5))
SPAN = {"A": (0, 3), "B": (3, 4), "C": (7, 3)}
TILE = {"A": 0, "B": 1, "C": 2}
COPIES = (("B", -1), ("B", 1), ("A", -1), ("C", 1), ("A", -2), ("C", 2))


def kernel(n_row, n_col, n_layer, cols_ref, signs_ref, blk_ref, out_ref, tr_ref, own, left1, left2, right1, right2, high, low,
           acc, flip, zero, mine, tb0, tb1, tb2, tb3, gsend, grecv, hsend, hrecv, osend, orecv, zsem, t0s, t0r, t1s, t1r, t2s, t2r,
           t3s, t3r):
    row, col, layer = lax.axis_index("row"), lax.axis_index("col"), lax.axis_index("layer")
    i32 = jnp.int32
    core = lax.rem(col, 2)
    base = 4 * core
    u = jnp.where(layer < base, layer - base + n_layer, layer - base)
    collector = (u == 1) | (u == 3)
    b = jnp.where(u == 3, 1, 0)
    first = (row == 0) & (col == 0)
    last = (row == n_row - 1) & (col == n_col - 1)
    wrap_up, wrap_down = col == n_col - 1, col == 0
    up = (jnp.where(wrap_up, jnp.where(row == n_row - 1, 0, row + 1), row), jnp.where(wrap_up, 0, col + 1))
    down = (jnp.where(wrap_down, jnp.where(row == 0, n_row - 1, row - 1), row), jnp.where(wrap_down, n_col - 1, col - 1))
    here = (row, col)
    far = 4 - base

    def pick(cond, x, y):
        return tuple(jnp.where(cond, p, q) for p, q in zip(x, y))

    peer = {
        1: pick(b == 0, (*here, base + 3), (*up, far + 1)),
        2: (*up, far + 1 + 2 * b),
        -1: pick(b == 0, (*down, far + 3), (*here, base + 1)),
        -2: (*down, far + 1 + 2 * b),
    }
    slot_up = jnp.where(first, 0, 1)
    slot_down = jnp.where(last, 1, 0)

    def turn(x, p, n):
        return jnp.where(x + p >= n, x + p - n, x + p)

    def remote(src, dst, send, recv, to):
        return pltpu.make_async_remote_copy(src, dst, send, recv, device_id=to, device_id_type=MESH)

    def arrived(ref, sem):
        pltpu.make_async_copy(ref, ref, sem).wait()

    others = [(row, col, turn(layer, p, n_layer)) for p in range(1, n_layer)]
    col_peers = [(row, turn(col, p, n_col), jnp.where(lax.rem(col + p, 2) == 0, 1, 5)) for p in range(1, n_col)]
    row_peers = [(turn(row, p, n_row), col, base + 1) for p in range(1, n_row)]

    barrier = pltpu.get_barrier_semaphore()

    def greet(to):
        pl.semaphore_signal(barrier, inc=1, device_id=to, device_id_type=MESH)

    @pl.when(collector)
    def _():
        for to in others:
            greet(to)

    for k in range(2):
        @pl.when(u != 1 + 2 * k)
        def _():
            greet((*here, base + 1 + 2 * k))

        greet((*down, far + 1 + 2 * k))

    @pl.when(collector)
    def _():
        for to in peer.values():
            greet(to)
        want = 1 + (n_layer - 1) + n_layer + 4

        @pl.when(b == 0)
        def _():
            for to in col_peers + row_peers:
                greet(to)
            pl.semaphore_wait(barrier, want + (n_col - 1) + (n_row - 1))

        @pl.when(b == 1)
        def _():
            pl.semaphore_wait(barrier, want)

    @pl.when(jnp.logical_not(collector))
    def _():
        pl.semaphore_wait(barrier, 2)

    def source(a):
        d = u - a
        q = u - 2 * (a // 2)
        two, four = jnp.where(q >= 2, 1, 0), jnp.where(q >= 4, 1, 0)
        n = q + 1 + 2 * two + four if a % 2 else q + two + 2 * four
        slot = jnp.where(d == ROWS, slot_up, 0)
        has = (d >= 0) & (d <= ROWS)
        return has, blk_ref.at[a, slot], n, (*here, base + 1 + 2 * (a // 2)), u == 1 + 2 * (a // 2)

    for a in range(ROWS):
        has, block, n, to, local = source(a)

        @pl.when(has & jnp.logical_not(local))
        def _():
            remote(block, own.at[0, n], gsend.at[a], grecv.at[n], to).start()

        @pl.when(has & local)
        def _():
            pltpu.make_async_copy(block, own.at[0, n], grecv.at[n]).start()

    zero[...] = jnp.zeros_like(zero)
    for a in range(ROWS):
        @pl.when(u != a + ROWS)
        def _():
            pltpu.make_async_copy(zero, out_ref.at[a, 1], zsem.at[a]).start()

    def landing(k, t):
        tile, to = COPIES[k]
        if to == 2:
            return left2.at[t]
        if to == -2:
            return right2.at[t]
        start, size = SPAN[tile]
        return left1.at[t, pl.ds(start - 3, size)] if to == 1 else right1.at[t, pl.ds(start, size)]

    def copy(k, t):
        tile, to = COPIES[k]
        start, size = SPAN[tile]
        return remote(own.at[t, pl.ds(start, size)], landing(k, t), hsend.at[t, k], hrecv.at[t, k], peer[to])

    def await_halo(k, t):
        arrived(landing(k, t), hrecv.at[t, k])

    def put(r, k, x):
        h = x.astype(jnp.bfloat16)
        lo = (x - h.astype(jnp.float32)).astype(jnp.bfloat16)
        high[r * B:(r + 1) * B, (k + 4) * B:(k + 5) * B] = h
        low[r * B:(r + 1) * B, (k + 4) * B:(k + 5) * B] = lo

    def put_both(r, k, x):
        put(r, k, x)
        if k > r:
            put(k, r, x.T)

    def product(tile, start, stop):
        j = 2 * TILE[tile]

        def part(ref, r):
            return ref[r * B:(r + 2) * B, (start + 4) * B:(stop + 4) * B]

        def dot(x, y):
            return lax.dot_general(x, y, (((1,), (1,)), ((), ())), preferred_element_type=jnp.float32)

        ah, al, bh, bl = part(high, 0), part(low, 0), part(high, j), part(low, j)
        return dot(ah, bh) + (dot(al, bh) + dot(ah, bl))

    def there(a, q):
        at_row = ROWS * (row * n_col + col) + 2 * b + a
        at_col = at_row + q - a
        slot = 2 * turn(base + 2 * b, q, n_layer)
        return (cols_ref[slot, at_row] == at_col) | (cols_ref[slot + 1, at_row] == at_col)

    def finish(t, tile, total):
        square = signs_ref[t] == 1
        keep = jnp.where(square, 0.0, 2.0).astype(jnp.float32)
        sign = jnp.where(square, 1.0, -1.0).astype(jnp.float32)
        start, size = SPAN[tile]
        for n in range(start, start + size):
            a, q = BLOCKS[n]
            factor = jnp.where(there(a, q), sign, 0.0)
            part = total[a * B:(a + 1) * B, (q % 2) * B:(q % 2 + 1) * B]
            own[t + 1, n] = keep * own[t, n] + factor * part

    def results(tile):
        start, size = SPAN[tile]
        for n in range(start, start + size):
            a, q = BLOCKS[n]
            slot = slot_up if q - a == ROWS else 0
            dst = out_ref.at[2 * b + a, slot]
            sem = orecv.at[2 * b + a, slot]
            src = own.at[STEPS, n]
            yield src, dst, osend.at[0, n], sem, (*here, turn(base + 2 * b, q, n_layer)), q == 1
            if q > a:
                over = 2 * b + q >= ROWS
                r = jnp.where(over, 2 * b + q - ROWS, 2 * b + q)
                slot = slot_down if q - a == ROWS else 0
                to = pick(over, up, here)
                local = (b == 0) if a == 1 and q < ROWS else False
                yield flip.at[n], out_ref.at[r, slot], osend.at[1, n], orecv.at[r, slot], (*to, base + 2 * b + a), local

    def deliver(tile):
        start, size = SPAN[tile]
        for n in range(start, start + size):
            a, q = BLOCKS[n]
            if q > a:
                flip[n] = own[STEPS, n].T
        for src, dst, send, recv, to, local in results(tile):
            if local is not True:
                @pl.when(jnp.logical_not(local))
                def _():
                    remote(src, dst, send, recv, to).start()
            if local is not False:
                @pl.when(local)
                def _():
                    pltpu.make_async_copy(src, dst, recv).start()

    def delivered(tile):
        for src, dst, send, recv, to, local in results(tile):
            if local is not True:
                @pl.when(jnp.logical_not(local))
                def _():
                    remote(src, dst, send, recv, to).wait_send()

    def share_pair():
        eye = lax.broadcasted_iota(i32, (B, B), 0) == lax.broadcasted_iota(i32, (B, B), 1)

        def diagonal(t):
            return jnp.sum(jnp.where(eye, own[t, 0] + own[t, 2], 0.0), axis=0, keepdims=True)

        one, two = diagonal(1), diagonal(2)
        diag = jnp.zeros((B, B), jnp.float32)
        off = jnp.zeros((B, B), jnp.float32)
        for n, (a, q) in enumerate(BLOCKS):
            x = own[2, n]
            if q > a:
                off = off + x * x
            else:
                diag = diag + x * x
        norm = jnp.sum(diag + 2.0 * off, axis=0, keepdims=True)
        three = jnp.where(signs_ref[2] == 1, norm, 2.0 * two - norm)
        line = lax.broadcasted_iota(i32, (8, B), 0)
        mine[...] = jnp.where(line == 0, one, jnp.where(line == 1, two, jnp.where(line == 2, three, 0.0)))

        @pl.when(b == 1)
        def _():
            remote(mine, tb0, t0s, t0r, (*here, base + 1)).start()

    def share_cols():
        arrived(tb0, t0r)
        tb1[col] = mine[...] + tb0[...]
        for p, to in enumerate(col_peers):
            remote(tb1.at[col], tb1.at[col], t1s.at[p], t1r.at[col], to).start()

    def share_rows():
        for p in range(1, n_col):
            c = turn(col, p, n_col)
            arrived(tb1.at[c], t1r.at[c])
        tb2[row] = jnp.sum(tb1[...], axis=0)
        for p, to in enumerate(row_peers):
            remote(tb2.at[row], tb2.at[row], t2s.at[p], t2r.at[row], to).start()

    def share_layers():
        for p in range(1, n_row):
            r = turn(row, p, n_row)
            arrived(tb2.at[r], t2r.at[r])
        total = jnp.sum(jnp.sum(tb2[...], axis=0), axis=1, keepdims=True) / (n_row * n_col * ROWS * B)
        mine[...] = jnp.broadcast_to(total, (8, B))
        for p, to in enumerate(others):
            remote(mine, tb3, t3s.at[p], t3r, to).start()

    @pl.when(collector)
    def _():
        for r, k in ((0, 5), (1, -4), (3, -2), (5, 0)):
            put(r, k, jnp.zeros((B, B), jnp.float32))
        for tile, ks in (("B", (0, 1)), ("A", (2, 4)), ("C", (3, 5))):
            start, size = SPAN[tile]
            for n in range(start, start + size):
                arrived(own.at[0, n], grecv.at[n])
            for k in ks:
                copy(k, 0).start()

        def step(t, carry):
            for n, (a, q) in enumerate(BLOCKS):
                put_both(a, q, own[t, n])
            pl.when(t == 2)(share_pair)
            acc[0] = product("A", 0, 6)
            acc[1] = product("B", 0, 2)
            acc[2] = product("C", 0, 2)
            pl.when((t == 2) & (b == 0))(share_cols)

            def after(tile, ks):
                @pl.when(t < 2)
                def _():
                    for k in ks:
                        copy(k, t + 1).start()

                @pl.when(t == 2)
                def _():
                    deliver(tile)

            await_halo(1, t)
            await_halo(3, t)
            for n in range(3, 10):
                a, q = BLOCKS[n]
                put(q - 2, a - 2, left1[t, n - 3].T)
            await_halo(0, t)
            await_halo(2, t)
            for n in range(7):
                a, q = BLOCKS[n]
                put_both(a + 2, q + 2, right1[t, n])
            finish(t, "B", acc[1] + product("B", -2, 0) + product("B", 2, 6))
            after("B", (0, 1))
            await_halo(5, t)
            for n in range(7, 10):
                a, q = BLOCKS[n]
                put(q - 4, a - 4, left2[t, n - 7].T)
            finish(t, "A", acc[0] + product("A", -4, 0))
            after("A", (2, 4))
            await_halo(4, t)
            for n in range(3):
                a, q = BLOCKS[n]
                put_both(a + 4, q + 4, right2[t, n])
            finish(t, "C", acc[2] + product("C", 2, 6))
            after("C", (3, 5))
            return carry

        lax.fori_loop(0, STEPS, step, 0)

        @pl.when(b == 0)
        def _():
            share_rows()
            share_layers()

        for t in range(STEPS):
            for k in range(len(COPIES)):
                copy(k, t).wait_send()
        for tile in SPAN:
            delivered(tile)

        @pl.when(b == 0)
        def _():
            for p, to in enumerate(col_peers):
                remote(tb1.at[col], tb1.at[col], t1s.at[p], t1r.at[col], to).wait_send()
            for p, to in enumerate(row_peers):
                remote(tb2.at[row], tb2.at[row], t2s.at[p], t2r.at[row], to).wait_send()
            for p, to in enumerate(others):
                remote(mine, tb3, t3s.at[p], t3r, to).wait_send()
            tb3[...] = mine[...]

        @pl.when(b == 1)
        def _():
            remote(mine, tb0, t0s, t0r, (*here, base + 1)).wait_send()

    for a in range(ROWS):
        has, block, n, to, local = source(a)

        @pl.when(has & jnp.logical_not(local))
        def _():
            remote(block, own.at[0, n], gsend.at[a], grecv.at[n], to).wait_send()

    @pl.when(u != 1)
    def _():
        arrived(tb3, t3r)

    for t in range(STEPS):
        tr_ref[t] = tb3[t, 0]
    for a in range(ROWS):
        arrived(out_ref.at[a, 0], orecv.at[a, 0])

        @pl.when(u == a + ROWS)
        def _():
            arrived(out_ref.at[a, 1], orecv.at[a, 1])

        @pl.when(u != a + ROWS)
        def _():
            pltpu.make_async_copy(zero, out_ref.at[a, 1], zsem.at[a]).wait()


def solution(mesh):
    n_row, n_col, n_layer = (mesh.shape[name] for name in ("row", "col", "layer"))
    dma = pltpu.SemaphoreType.DMA

    def shards(blocks, columns, signs):
        def body(*refs):
            kernel(n_row, n_col, n_layer, *refs)

        f32, bf16 = jnp.float32, jnp.bfloat16
        return pl.pallas_call(
            body,
            out_shape=(jax.ShapeDtypeStruct(blocks.shape, f32), jax.ShapeDtypeStruct((STEPS,), f32)),
            in_specs=[
                pl.BlockSpec(memory_space=pltpu.SMEM),
                pl.BlockSpec(memory_space=pltpu.SMEM),
                pl.BlockSpec(memory_space=pl.ANY),
            ],
            out_specs=(pl.BlockSpec(memory_space=pl.ANY), pl.BlockSpec(memory_space=pltpu.SMEM)),
            scratch_shapes=[
                pltpu.VMEM((STEPS + 1, 10, B, B), f32),
                pltpu.VMEM((STEPS, 7, B, B), f32),
                pltpu.VMEM((STEPS, 3, B, B), f32),
                pltpu.VMEM((STEPS, 7, B, B), f32),
                pltpu.VMEM((STEPS, 3, B, B), f32),
                pltpu.VMEM((6 * B, 10 * B), bf16),
                pltpu.VMEM((6 * B, 10 * B), bf16),
                pltpu.VMEM((3, 2 * B, 2 * B), f32),
                pltpu.VMEM((10, B, B), f32),
                pltpu.VMEM((B, B), f32),
                pltpu.VMEM((8, B), f32),
                pltpu.VMEM((8, B), f32),
                pltpu.VMEM((n_col, 8, B), f32),
                pltpu.VMEM((n_row, 8, B), f32),
                pltpu.VMEM((8, B), f32),
                dma((ROWS,)),
                dma((10,)),
                dma((STEPS, len(COPIES))),
                dma((STEPS, len(COPIES))),
                dma((2, 10)),
                dma((ROWS, 2)),
                dma((ROWS,)),
                dma,
                dma,
                dma((n_col,)),
                dma((n_col,)),
                dma((n_row,)),
                dma((n_row,)),
                dma((n_layer,)),
                dma,
            ],
            compiler_params=pltpu.CompilerParams(
                collective_id=0, has_side_effects=True, vmem_limit_bytes=60 * 1024 * 1024
            ),
        )(columns.T, signs, blocks)

    return jax.shard_map(
        shards,
        mesh=mesh,
        in_specs=(P(("row", "col"), "layer", None, None), P(), P()),
        out_specs=(P(("row", "col"), "layer", None, None), P()),
        check_vma=False,
    )
```

```python
import jax
import jax.numpy as jnp
from jax import lax
from jax.experimental import pallas as pl
from jax.experimental.pallas import tpu as pltpu
from jax.sharding import PartitionSpec as P

MESH = pl.DeviceIdType.MESH
B = 128
ROWS = 4
STEPS = 3
BLOCKS = ((0, 0), (0, 1), (1, 1), (0, 2), (0, 3), (1, 2), (1, 3), (0, 4), (1, 4), (1, 5))
SPAN = {"A": (0, 3), "B": (3, 4), "C": (7, 3)}
TILE = {"A": 0, "B": 1, "C": 2}
COPIES = (("B", -1), ("B", 1), ("A", -1), ("C", 1), ("A", -2), ("C", 2))
DOWN_B, UP_B, DOWN_A, UP_C, PASS_A, PASS_C = range(6)


def kernel(n_row, n_col, n_layer, cols_ref, signs_ref, blk_ref, out_ref, tr_ref, own, left1, left2, right1, right2, high, low,
           acc, flip, zero, mine, tb1, tb2, tb3, gsend, grecv, hsend, hrecv, osend, orecv, zsem, t1s, t1r, t2s, t2r, t3s,
           t3r):
    row, col, layer = lax.axis_index("row"), lax.axis_index("col"), lax.axis_index("layer")
    i32 = jnp.int32
    core = lax.rem(col, 2)
    base = 4 * core
    u = jnp.where(layer < base, layer - base + n_layer, layer - base)
    collector = (u == 1) | (u == 3)
    b = jnp.where(u == 3, 1, 0)
    first = (row == 0) & (col == 0)
    last = (row == n_row - 1) & (col == n_col - 1)
    wrap_up, wrap_down = col == n_col - 1, col == 0
    up = (jnp.where(wrap_up, jnp.where(row == n_row - 1, 0, row + 1), row), jnp.where(wrap_up, 0, col + 1))
    down = (jnp.where(wrap_down, jnp.where(row == 0, n_row - 1, row - 1), row), jnp.where(wrap_down, n_col - 1, col - 1))
    here = (row, col)
    far = 4 - base

    def pick(cond, x, y):
        return tuple(jnp.where(cond, p, q) for p, q in zip(x, y))

    peer = {
        1: pick(b == 0, (*here, base + 3), (*up, far + 1)),
        -1: pick(b == 0, (*down, far + 3), (*here, base + 1)),
    }
    slot_up = jnp.where(first, 0, 1)
    slot_down = jnp.where(last, 1, 0)

    def turn(x, p, n):
        return jnp.where(x + p >= n, x + p - n, x + p)

    def remote(src, dst, send, recv, to):
        return pltpu.make_async_remote_copy(src, dst, send, recv, device_id=to, device_id_type=MESH)

    def arrived(ref, sem):
        pltpu.make_async_copy(ref, ref, sem).wait()

    others = [(row, col, turn(layer, p, n_layer)) for p in range(1, n_layer)]
    col_peers = [(row, turn(col, p, n_col), (far if p % 2 else base) + 1 + 2 * b) for p in range(1, n_col)]
    row_peers = [(turn(row, p, n_row), col, layer) for p in range(1, n_row)]

    barrier = pltpu.get_barrier_semaphore()

    def greet(to):
        pl.semaphore_signal(barrier, inc=1, device_id=to, device_id_type=MESH)

    @pl.when(collector)
    def _():
        for to in others:
            greet(to)

    for k in range(2):
        @pl.when(u != 1 + 2 * k)
        def _():
            greet((*here, base + 1 + 2 * k))

        greet((*down, far + 1 + 2 * k))

    @pl.when(collector)
    def _():
        for to in [*peer.values(), *col_peers, *row_peers]:
            greet(to)
        pl.semaphore_wait(barrier, 1 + (n_layer - 1) + n_layer + 2 + (n_col - 1) + (n_row - 1))

    @pl.when(jnp.logical_not(collector))
    def _():
        pl.semaphore_wait(barrier, 2)

    def source(a):
        d = u - a
        q = u - 2 * (a // 2)
        two, four = jnp.where(q >= 2, 1, 0), jnp.where(q >= 4, 1, 0)
        n = q + 1 + 2 * two + four if a % 2 else q + two + 2 * four
        slot = jnp.where(d == ROWS, slot_up, 0)
        has = (d >= 0) & (d <= ROWS)
        return has, blk_ref.at[a, slot], n, (*here, base + 1 + 2 * (a // 2)), u == 1 + 2 * (a // 2)

    for a in range(ROWS):
        has, block, n, to, local = source(a)

        @pl.when(has & jnp.logical_not(local))
        def _():
            remote(block, own.at[0, n], gsend.at[a], grecv.at[n], to).start()

        @pl.when(has & local)
        def _():
            pltpu.make_async_copy(block, own.at[0, n], grecv.at[n]).start()

    zero[...] = jnp.zeros_like(zero)
    for a in range(ROWS):
        @pl.when(u != a + ROWS)
        def _():
            pltpu.make_async_copy(zero, out_ref.at[a, 1], zsem.at[a]).start()

    def landing(k, t):
        tile, come = COPIES[k]
        if come == 2:
            return left2.at[t]
        if come == -2:
            return right2.at[t]
        start, size = SPAN[tile]
        return left1.at[t, pl.ds(start - 3, size)] if come == 1 else right1.at[t, pl.ds(start, size)]

    def copy(k, t):
        tile, come = COPIES[k]
        start, size = SPAN[tile]
        src = {PASS_A: landing(DOWN_A, t), PASS_C: landing(UP_C, t)}.get(k, own.at[t, pl.ds(start, size)])
        return remote(src, landing(k, t), hsend.at[t, k], hrecv.at[t, k], peer[1 if come > 0 else -1])

    def await_halo(k, t):
        arrived(landing(k, t), hrecv.at[t, k])

    def put(r, k, x):
        h = x.astype(jnp.bfloat16)
        lo = (x - h.astype(jnp.float32)).astype(jnp.bfloat16)
        high[r * B:(r + 1) * B, (k + 4) * B:(k + 5) * B] = h
        low[r * B:(r + 1) * B, (k + 4) * B:(k + 5) * B] = lo

    def put_both(r, k, x):
        put(r, k, x)
        if k > r:
            put(k, r, x.T)

    def product(tile, start, stop):
        j = 2 * TILE[tile]

        def part(ref, r):
            return ref[r * B:(r + 2) * B, (start + 4) * B:(stop + 4) * B]

        def dot(x, y):
            return lax.dot_general(x, y, (((1,), (1,)), ((), ())), preferred_element_type=jnp.float32)

        ah, al, bh, bl = part(high, 0), part(low, 0), part(high, j), part(low, j)
        return dot(ah, bh) + (dot(al, bh) + dot(ah, bl))

    def there(a, q):
        at_row = ROWS * (row * n_col + col) + 2 * b + a
        at_col = at_row + q - a
        slot = 2 * turn(base + 2 * b, q, n_layer)
        return (cols_ref[slot, at_row] == at_col) | (cols_ref[slot + 1, at_row] == at_col)

    def finish(t, tile, total):
        square = signs_ref[t] == 1
        keep = jnp.where(square, 0.0, 2.0).astype(jnp.float32)
        sign = jnp.where(square, 1.0, -1.0).astype(jnp.float32)
        start, size = SPAN[tile]
        for n in range(start, start + size):
            a, q = BLOCKS[n]
            factor = jnp.where(there(a, q), sign, 0.0)
            part = total[a * B:(a + 1) * B, (q % 2) * B:(q % 2 + 1) * B]
            own[t + 1, n] = keep * own[t, n] + factor * part

    def results(tile):
        start, size = SPAN[tile]
        for n in range(start, start + size):
            a, q = BLOCKS[n]
            slot = slot_up if q - a == ROWS else 0
            dst = out_ref.at[2 * b + a, slot]
            sem = orecv.at[2 * b + a, slot]
            src = own.at[STEPS, n]
            yield src, dst, osend.at[0, n], sem, (*here, turn(base + 2 * b, q, n_layer)), q == 1
            if q > a:
                over = 2 * b + q >= ROWS
                r = jnp.where(over, 2 * b + q - ROWS, 2 * b + q)
                slot = slot_down if q - a == ROWS else 0
                to = pick(over, up, here)
                local = (b == 0) if a == 1 and q < ROWS else False
                yield flip.at[n], out_ref.at[r, slot], osend.at[1, n], orecv.at[r, slot], (*to, base + 2 * b + a), local

    def deliver(tile):
        start, size = SPAN[tile]
        for n in range(start, start + size):
            a, q = BLOCKS[n]
            if q > a:
                flip[n] = own[STEPS, n].T
        for src, dst, send, recv, to, local in results(tile):
            if local is not True:
                @pl.when(jnp.logical_not(local))
                def _():
                    remote(src, dst, send, recv, to).start()
            if local is not False:
                @pl.when(local)
                def _():
                    pltpu.make_async_copy(src, dst, recv).start()

    def delivered(tile):
        for src, dst, send, recv, to, local in results(tile):
            if local is not True:
                @pl.when(jnp.logical_not(local))
                def _():
                    remote(src, dst, send, recv, to).wait_send()

    def share_cols():
        eye = lax.broadcasted_iota(i32, (B, B), 0) == lax.broadcasted_iota(i32, (B, B), 1)

        def diagonal(t):
            return jnp.sum(jnp.where(eye, own[t, 0] + own[t, 2], 0.0), axis=0, keepdims=True)

        one, two = diagonal(1), diagonal(2)
        diag = jnp.zeros((B, B), jnp.float32)
        off = jnp.zeros((B, B), jnp.float32)
        for n, (a, q) in enumerate(BLOCKS):
            x = own[2, n]
            if q > a:
                off = off + x * x
            else:
                diag = diag + x * x
        norm = jnp.sum(diag + 2.0 * off, axis=0, keepdims=True)
        three = jnp.where(signs_ref[2] == 1, norm, 2.0 * two - norm)
        line = lax.broadcasted_iota(i32, (8, B), 0)
        tb1[col] = jnp.where(line == 0, one, jnp.where(line == 1, two, jnp.where(line == 2, three, 0.0)))
        for p, to in enumerate(col_peers):
            remote(tb1.at[col], tb1.at[col], t1s.at[p], t1r.at[col], to).start()

    def share_rows():
        for p in range(1, n_col):
            c = turn(col, p, n_col)
            arrived(tb1.at[c], t1r.at[c])
        tb2[row] = jnp.sum(tb1[...], axis=0)
        for p, to in enumerate(row_peers):
            remote(tb2.at[row], tb2.at[row], t2s.at[p], t2r.at[row], to).start()

    def share_layers():
        for p in range(1, n_row):
            r = turn(row, p, n_row)
            arrived(tb2.at[r], t2r.at[r])
        total = jnp.sum(jnp.sum(tb2[...], axis=0), axis=1, keepdims=True) / (n_row * n_col * ROWS * B)
        mine[...] = jnp.broadcast_to(total, (8, B))
        for p, to in enumerate(others):
            remote(mine, tb3.at[b], t3s.at[p], t3r.at[b], to).start()

    @pl.when(collector)
    def _():
        for r, k in ((0, 5), (1, -4), (3, -2), (5, 0)):
            put(r, k, jnp.zeros((B, B), jnp.float32))
        for tile, ks in (("C", (UP_C,)), ("A", (DOWN_A,)), ("B", (UP_B, DOWN_B))):
            start, size = SPAN[tile]
            for n in range(start, start + size):
                arrived(own.at[0, n], grecv.at[n])
            for k in ks:
                copy(k, 0).start()

        def step(t, carry):
            pl.when(t == 2)(share_cols)
            for n, (a, q) in enumerate(BLOCKS):
                put_both(a, q, own[t, n])
            acc[0] = product("A", 0, 6)
            acc[1] = product("B", 0, 2)
            acc[2] = product("C", 0, 2)

            def after(tile, *ks):
                @pl.when(t < 2)
                def _():
                    for k in ks:
                        copy(k, t + 1).start()

                @pl.when(t == 2)
                def _():
                    deliver(tile)

            await_halo(UP_C, t)
            copy(PASS_C, t).start()
            await_halo(DOWN_A, t)
            copy(PASS_A, t).start()
            pl.when(t == 2)(share_rows)
            for n in range(7, 10):
                a, q = BLOCKS[n]
                put(q - 2, a - 2, left1[t, n - 3].T)
            for n in range(3):
                a, q = BLOCKS[n]
                put_both(a + 2, q + 2, right1[t, n])
            await_halo(UP_B, t)
            await_halo(DOWN_B, t)
            for n in range(3, 7):
                a, q = BLOCKS[n]
                put(q - 2, a - 2, left1[t, n - 3].T)
                put_both(a + 2, q + 2, right1[t, n])
            finish(t, "B", acc[1] + product("B", -2, 0) + product("B", 2, 6))
            pl.when(t == 2)(share_layers)
            after("B", UP_B, DOWN_B)
            await_halo(PASS_C, t)
            for n in range(7, 10):
                a, q = BLOCKS[n]
                put(q - 4, a - 4, left2[t, n - 7].T)
            finish(t, "A", acc[0] + product("A", -4, 0))
            after("A", DOWN_A)
            await_halo(PASS_A, t)
            for n in range(3):
                a, q = BLOCKS[n]
                put_both(a + 4, q + 4, right2[t, n])
            finish(t, "C", acc[2] + product("C", 2, 6))
            after("C", UP_C)
            return carry

        lax.fori_loop(0, STEPS, step, 0)

        for t in range(STEPS):
            for k in range(len(COPIES)):
                copy(k, t).wait_send()
        for tile in SPAN:
            delivered(tile)

        for p, to in enumerate(col_peers):
            remote(tb1.at[col], tb1.at[col], t1s.at[p], t1r.at[col], to).wait_send()
        for p, to in enumerate(row_peers):
            remote(tb2.at[row], tb2.at[row], t2s.at[p], t2r.at[row], to).wait_send()
        for p, to in enumerate(others):
            remote(mine, tb3.at[b], t3s.at[p], t3r.at[b], to).wait_send()
        tb3[b] = mine[...]

    for a in range(ROWS):
        has, block, n, to, local = source(a)

        @pl.when(has & jnp.logical_not(local))
        def _():
            remote(block, own.at[0, n], gsend.at[a], grecv.at[n], to).wait_send()

    for k in range(2):
        @pl.when(u != 1 + 2 * k)
        def _():
            arrived(tb3.at[k], t3r.at[k])

    for t in range(STEPS):
        tr_ref[t] = tb3[0, t, 0] + tb3[1, t, 0]
    for a in range(ROWS):
        arrived(out_ref.at[a, 0], orecv.at[a, 0])

        @pl.when(u == a + ROWS)
        def _():
            arrived(out_ref.at[a, 1], orecv.at[a, 1])

        @pl.when(u != a + ROWS)
        def _():
            pltpu.make_async_copy(zero, out_ref.at[a, 1], zsem.at[a]).wait()


def solution(mesh):
    n_row, n_col, n_layer = (mesh.shape[name] for name in ("row", "col", "layer"))
    dma = pltpu.SemaphoreType.DMA

    def shards(blocks, columns, signs):
        def body(*refs):
            kernel(n_row, n_col, n_layer, *refs)

        f32, bf16 = jnp.float32, jnp.bfloat16
        return pl.pallas_call(
            body,
            out_shape=(jax.ShapeDtypeStruct(blocks.shape, f32), jax.ShapeDtypeStruct((STEPS,), f32)),
            in_specs=[
                pl.BlockSpec(memory_space=pltpu.SMEM),
                pl.BlockSpec(memory_space=pltpu.SMEM),
                pl.BlockSpec(memory_space=pltpu.HBM),
            ],
            out_specs=(pl.BlockSpec(memory_space=pl.ANY), pl.BlockSpec(memory_space=pltpu.SMEM)),
            scratch_shapes=[
                pltpu.VMEM((STEPS + 1, 10, B, B), f32),
                pltpu.VMEM((STEPS, 7, B, B), f32),
                pltpu.VMEM((STEPS, 3, B, B), f32),
                pltpu.VMEM((STEPS, 7, B, B), f32),
                pltpu.VMEM((STEPS, 3, B, B), f32),
                pltpu.VMEM((6 * B, 10 * B), bf16),
                pltpu.VMEM((6 * B, 10 * B), bf16),
                pltpu.VMEM((3, 2 * B, 2 * B), f32),
                pltpu.VMEM((10, B, B), f32),
                pltpu.VMEM((B, B), f32),
                pltpu.VMEM((8, B), f32),
                pltpu.VMEM((n_col, 8, B), f32),
                pltpu.VMEM((n_row, 8, B), f32),
                pltpu.VMEM((2, 8, B), f32),
                dma((ROWS,)),
                dma((10,)),
                dma((STEPS, len(COPIES))),
                dma((STEPS, len(COPIES))),
                dma((2, 10)),
                dma((ROWS, 2)),
                dma((ROWS,)),
                dma((n_col,)),
                dma((n_col,)),
                dma((n_row,)),
                dma((n_row,)),
                dma((n_layer,)),
                dma((2,)),
            ],
            compiler_params=pltpu.CompilerParams(
                collective_id=0, has_side_effects=True, vmem_limit_bytes=48 * 1024 * 1024
            ),
        )(columns.T, signs, blocks)

    return jax.shard_map(
        shards,
        mesh=mesh,
        in_specs=(P(("row", "col"), "layer", None, None), P(), P()),
        out_specs=(P(("row", "col"), "layer", None, None), P()),
        check_vma=False,
    )
```

```python
import jax
import jax.numpy as jnp
from jax import lax
from jax.experimental import pallas as pl
from jax.experimental.pallas import tpu as pltpu
from jax.sharding import PartitionSpec as P

MESH = pl.DeviceIdType.MESH
B = 128
ROWS = 4
STEPS = 3
BLOCKS = ((0, 0), (0, 1), (1, 1), (0, 2), (0, 3), (1, 2), (1, 3), (-2, 2), (-1, 2), (-1, 3))
SPAN = {"A": (0, 3), "B": (3, 4), "D": (7, 3)}
CORNER = {"A": (0, 0), "B": (0, 2), "D": (-2, 2)}
UP, DOWN = 1, -1


def kernel(n_row, n_col, n_layer, cols_ref, signs_ref, blk_ref, out_ref, tr_ref, own, left, right, high, low, acc,
           flip, zero, mine, tb1, tb2, tb3, gsend, grecv, hsend, hrecv, osend, orecv, zsem, t1s, t1r, t2s, t2r, t3s,
           t3r):
    row, col, layer = lax.axis_index("row"), lax.axis_index("col"), lax.axis_index("layer")
    i32 = jnp.int32
    core = lax.rem(col, 2)
    base = 4 * core
    u = jnp.where(layer < base, layer - base + n_layer, layer - base)
    collector = (u == 1) | (u == 3)
    b = jnp.where(u == 3, 1, 0)
    first = (row == 0) & (col == 0)
    last = (row == n_row - 1) & (col == n_col - 1)
    wrap_up, wrap_down = col == n_col - 1, col == 0
    up = (jnp.where(wrap_up, jnp.where(row == n_row - 1, 0, row + 1), row), jnp.where(wrap_up, 0, col + 1))
    down = (jnp.where(wrap_down, jnp.where(row == 0, n_row - 1, row - 1), row), jnp.where(wrap_down, n_col - 1, col - 1))
    here = (row, col)
    far = 4 - base

    def pick(cond, x, y):
        return tuple(jnp.where(cond, p, q) for p, q in zip(x, y))

    peer = {
        1: pick(b == 0, (*here, base + 3), (*up, far + 1)),
        -1: pick(b == 0, (*down, far + 3), (*here, base + 1)),
    }
    slot_up = jnp.where(first, 0, 1)
    slot_up_before = jnp.where((row == 0) & (col == 1), 0, 1)
    slot_down = jnp.where(first, 1, 0)
    slot_down_after = jnp.where(last, 1, 0)

    def turn(x, p, n):
        return jnp.where(x + p >= n, x + p - n, x + p)

    def remote(src, dst, send, recv, to):
        return pltpu.make_async_remote_copy(src, dst, send, recv, device_id=to, device_id_type=MESH)

    def arrived(ref, sem):
        pltpu.make_async_copy(ref, ref, sem).wait()

    others = [(row, col, turn(layer, p, n_layer)) for p in range(1, n_layer)]
    col_peers = [(row, turn(col, p, n_col), (far if p % 2 else base) + 1 + 2 * b) for p in range(1, n_col)]
    row_peers = [(turn(row, p, n_row), col, layer) for p in range(1, n_row)]

    barrier = pltpu.get_barrier_semaphore()

    def greet(to):
        pl.semaphore_signal(barrier, inc=1, device_id=to, device_id_type=MESH)

    def ready(group, start, columns):
        for k in columns:
            greet((*group, turn(start, k, n_layer)))

    @pl.when(u == 1)
    def _():
        ready(here, base, (0, 2, 3))
        ready(down, far, (2, 3, 4, 5, 6, 7))
        ready(up, far, (4, 5, 6, 7))

    @pl.when(u == 3)
    def _():
        ready(here, base, (0, 1, 2, 4, 5))
        ready(down, far, (6, 7))
        ready(up, far, (0, 1, 6, 7))

    for k in range(2):
        @pl.when(u != 1 + 2 * k)
        def _():
            greet((*here, base + 1 + 2 * k))

    greet((*down, far + 3))
    greet((*up, far + 1))

    @pl.when(collector)
    def _():
        for to in [*peer.values(), *col_peers, *row_peers]:
            greet(to)
        pl.semaphore_wait(barrier, 2 + (n_layer - 1) + n_layer + 2 + (n_col - 1) + (n_row - 1))

    @pl.when(jnp.logical_not(collector) & (u < 6))
    def _():
        pl.semaphore_wait(barrier, 3)

    @pl.when(u >= 6)
    def _():
        pl.semaphore_wait(barrier, 4)

    def sources(a):
        pair, d, q = a // 2, u - a, u - 2 * (a // 2)
        two, four = jnp.where(q >= 2, 1, 0), jnp.where(q >= 4, 1, 0)
        n = q + 1 + 2 * two + four if a % 2 else q + two + 2 * four
        has = (d >= 0) & (d <= ROWS)
        block = blk_ref.at[a, jnp.where(d == ROWS, slot_up, 0)]
        mine_, next_ = (*here, base + 1 + 2 * pair), ((*here, base + 3) if a < 2 else (*up, far + 1))
        third = (*up, far + 1) if a < 2 else (*up, far + 3)
        yield has & (q < 2), block, right.at[0, n], grecv.at[2, n], (*down, far + 3) if a < 2 else (*here, base + 1), False
        yield has, block, left.at[0, n], grecv.at[1, n], pick(q >= 4, third, next_), u == 3 if a < 2 else False
        yield has, block, own.at[0, n], grecv.at[0, n], pick(q >= 4, next_, mine_), u == 1 + 2 * pair
        c = jnp.where(u < ROWS, u, u - n_layer) - 2 * pair + 2
        n = jnp.where(c >= 0, 3 + a % 2 + 2 * c, 9 + a % 2 + c)
        has = (u >= a + ROWS) | (u < 2) if a >= 2 else u >= a + ROWS
        block = blk_ref.at[a, jnp.where(u == a + ROWS, slot_down, 0)]
        yield has, block, right.at[0, n], grecv.at[2, n], (*down, far + 1 + 2 * pair), False

    plans = list(zip(*(sources(a) for a in range(ROWS))))
    for k, plan in enumerate(plans):
        for a, (has, block, dst, sem, to, local) in enumerate(plan):
            @pl.when(has & jnp.logical_not(local))
            def _():
                remote(block, dst, gsend.at[k, a], sem, to).start()

            if local is not False:
                @pl.when(has & local)
                def _():
                    pltpu.make_async_copy(block, dst, sem).start()

    zero[...] = jnp.zeros_like(zero)
    for a in range(ROWS):
        @pl.when(u != a + ROWS)
        def _():
            pltpu.make_async_copy(zero, out_ref.at[a, 1], zsem.at[a]).start()

    def copy(tile, way, t):
        part = pl.ds(*SPAN[tile])
        k = 2 * list(SPAN).index(tile) + (way == UP)
        dst = left if way == UP else right
        return remote(own.at[t, part], dst.at[t, part], hsend.at[t, k], hrecv.at[t, k], peer[way])

    def come(tile, way, t):
        part = pl.ds(*SPAN[tile])
        k = 2 * list(SPAN).index(tile) + (way == UP)
        dst = left if way == UP else right
        blocks = range(SPAN[tile][0], sum(SPAN[tile]))
        turned = way == DOWN and tile != "A"

        @pl.when(t == 0)
        def _():
            for n in blocks:
                arrived(dst.at[0, n], grecv.at[1 if way == UP else 2, n])
            if turned:
                for n in blocks:
                    a, q = BLOCKS[n]
                    put(a + 2, q + 2, dst[0, n].T)

        @pl.when(t > 0)
        def _():
            arrived(dst.at[t, part], hrecv.at[t, k])
            if turned:
                for n in blocks:
                    a, q = BLOCKS[n]
                    put(a + 2, q + 2, dst[t, n])

        if not turned:
            for n in blocks:
                a, q = BLOCKS[n]
                put_both(a - 2 * way, q - 2 * way, dst[t, n])

    def put(r, k, x):
        h = x.astype(jnp.bfloat16)
        lo = (x - h.astype(jnp.float32)).astype(jnp.bfloat16)
        high[(r + 2) * B:(r + 3) * B, (k + 4) * B:(k + 5) * B] = h
        low[(r + 2) * B:(r + 3) * B, (k + 4) * B:(k + 5) * B] = lo

    def put_both(r, k, x):
        if -2 <= r < 4:
            put(r, k, x)
        if k > r and -2 <= k < 4:
            put(k, r, x.T)

    def product(tile, start, stop):
        i, j = CORNER[tile]

        def part(ref, r):
            return ref[(r + 2) * B:(r + 4) * B, (start + 4) * B:(stop + 4) * B]

        def dot(x, y):
            return lax.dot_general(x, y, (((1,), (1,)), ((), ())), preferred_element_type=jnp.float32)

        ah, al, bh, bl = part(high, i), part(low, i), part(high, j), part(low, j)
        return dot(ah, bh) + (dot(al, bh) + dot(ah, bl))

    def there(a, q):
        at_row = ROWS * (row * n_col + col) + 2 * b + a
        at_col = at_row + q - a
        slot = 2 * turn(base + 2 * b, q, n_layer)
        r = jnp.maximum(at_row, 0)
        return (at_row >= 0) & ((cols_ref[slot, r] == at_col) | (cols_ref[slot + 1, r] == at_col))

    def finish(t, tile, total, masks):
        square = signs_ref[t] == 1
        keep = jnp.where(square, 0.0, 2.0).astype(jnp.float32)
        sign = jnp.where(square, 1.0, -1.0).astype(jnp.float32)
        start, size = SPAN[tile]
        for n in range(start, start + size):
            a, q = BLOCKS[n]
            factor = sign * masks[n]
            part = total[(a % 2) * B:(a % 2 + 1) * B, (q % 2) * B:(q % 2 + 1) * B]
            own[t + 1, n] = keep * own[t, n] + factor * part

    def results(tile):
        start, size = SPAN[tile]
        for n in range(start, start + size):
            a, q = BLOCKS[n]
            wide = q - a == ROWS
            at_a, at_q = turn(base + 2 * b, a % n_layer, n_layer), turn(base + 2 * b, q, n_layer)
            if a >= 0:
                group, r, slot = here, 2 * b + a, 0
            else:
                group = pick(b == 0, down, here)
                r = jnp.where(b == 0, ROWS + a, 2 + a)
                slot = jnp.where(b == 0, slot_up_before, slot_up) if wide else 0
            yield own.at[STEPS, n], out_ref.at[r, slot], osend.at[0, n], orecv.at[r, slot], (*group, at_q), q == 1
            if q > a:
                over = 2 * b + q >= ROWS
                group = pick(over, up, here)
                r = jnp.where(over, 2 * b + q - ROWS, 2 * b + q)
                slot = jnp.where(over, slot_down_after, slot_down) if wide else 0
                local = b == 0 if a == 1 else False
                yield flip.at[n], out_ref.at[r, slot], osend.at[1, n], orecv.at[r, slot], (*group, at_a), local

    def deliver(tile):
        start, size = SPAN[tile]
        for n in range(start, start + size):
            a, q = BLOCKS[n]
            if q > a:
                flip[n] = own[STEPS, n].T
        for src, dst, send, recv, to, local in results(tile):
            if local is not True:
                @pl.when(jnp.logical_not(local))
                def _():
                    remote(src, dst, send, recv, to).start()
            if local is not False:
                @pl.when(local)
                def _():
                    pltpu.make_async_copy(src, dst, recv).start()

    def delivered(tile):
        for src, dst, send, recv, to, local in results(tile):
            if local is not True:
                @pl.when(jnp.logical_not(local))
                def _():
                    remote(src, dst, send, recv, to).wait_send()

    def share_cols():
        eye = lax.broadcasted_iota(i32, (B, B), 0) == lax.broadcasted_iota(i32, (B, B), 1)

        def diagonal(t):
            return jnp.sum(jnp.where(eye, own[t, 0] + own[t, 2], 0.0), axis=0, keepdims=True)

        one, two = diagonal(1), diagonal(2)
        diag = jnp.zeros((B, B), jnp.float32)
        off = jnp.zeros((B, B), jnp.float32)
        for n, (a, q) in enumerate(BLOCKS):
            x = own[2, n]
            if q > a:
                off = off + x * x
            else:
                diag = diag + x * x
        norm = jnp.sum(diag + 2.0 * off, axis=0, keepdims=True)
        three = jnp.where(signs_ref[2] == 1, norm, 2.0 * two - norm)
        line = lax.broadcasted_iota(i32, (8, B), 0)
        tb1[col] = jnp.where(line == 0, one, jnp.where(line == 1, two, jnp.where(line == 2, three, 0.0)))
        for p, to in enumerate(col_peers):
            remote(tb1.at[col], tb1.at[col], t1s.at[p], t1r.at[col], to).start()

    def share_rows():
        for p in range(1, n_col):
            c = turn(col, p, n_col)
            arrived(tb1.at[c], t1r.at[c])
        tb2[row] = jnp.sum(tb1[...], axis=0)
        for p, to in enumerate(row_peers):
            remote(tb2.at[row], tb2.at[row], t2s.at[p], t2r.at[row], to).start()

    def share_layers():
        for p in range(1, n_row):
            r = turn(row, p, n_row)
            arrived(tb2.at[r], t2r.at[r])
        total = jnp.sum(jnp.sum(tb2[...], axis=0), axis=1, keepdims=True) / (n_row * n_col * ROWS * B)
        mine[...] = jnp.broadcast_to(total, (8, B))
        for p, to in enumerate(others):
            remote(mine, tb3.at[b], t3s.at[p], t3r.at[b], to).start()

    @pl.when(collector)
    def _():
        for r, k in ((0, 5), (1, -4), (3, -2), (-2, 3)):
            put(r, k, jnp.zeros((B, B), jnp.float32))
        masks = [jnp.where(there(a, q), 1.0, 0.0).astype(jnp.float32) for a, q in BLOCKS]

        for n in range(len(BLOCKS)):
            arrived(own.at[0, n], grecv.at[0, n])

        def step(t, carry):
            pl.when(t == 2)(share_cols)
            for n, (a, q) in enumerate(BLOCKS):
                put_both(a, q, own[t, n])
            acc[0] = product("A", 0, 4)
            acc[1] = product("B", 0, 2)

            def send(when, *copies):
                @pl.when(when)
                def _():
                    for tile, way in copies:
                        copy(tile, way, t + 1).start()

            def make_d(even):
                come("A", DOWN, t)
                come("A", UP, t)
                if even:
                    pl.when(t == 2)(share_rows)
                finish(t, "D", product("D", -2, 4), masks)
                if even:
                    send(t == 0, ("D", UP), ("D", DOWN))
                    pl.when(t == 2)(lambda: deliver("D"))
                else:
                    copy("D", DOWN, 2).start()

            come("B", UP, t)
            pl.when(t != 1)(lambda: make_d(True))
            come("D", DOWN, t)
            come("D", UP, t)
            finish(t, "A", acc[0] + product("A", -4, 0) + product("A", 4, 6), masks)
            send(t < 2, ("A", DOWN))
            send(t == 1, ("A", UP))
            pl.when(t == 2)(lambda: deliver("A"))
            pl.when(t == 1)(lambda: make_d(False))
            come("B", DOWN, t)
            finish(t, "B", acc[1] + product("B", -2, 0) + product("B", 2, 6), masks)
            send(t < 2, ("B", UP), ("B", DOWN))
            send(t == 0, ("A", UP))
            send(t == 1, ("D", UP))

            @pl.when(t == 2)
            def _():
                share_layers()
                deliver("B")

            return carry

        lax.fori_loop(0, STEPS, step, 0)

        for t in range(1, STEPS):
            for tile in SPAN:
                for way in (UP, DOWN):
                    copy(tile, way, t).wait_send()
        for tile in SPAN:
            delivered(tile)

        for p, to in enumerate(col_peers):
            remote(tb1.at[col], tb1.at[col], t1s.at[p], t1r.at[col], to).wait_send()
        for p, to in enumerate(row_peers):
            remote(tb2.at[row], tb2.at[row], t2s.at[p], t2r.at[row], to).wait_send()
        for p, to in enumerate(others):
            remote(mine, tb3.at[b], t3s.at[p], t3r.at[b], to).wait_send()
        tb3[b] = mine[...]

    for k, plan in enumerate(plans):
        for a, (has, block, dst, sem, to, local) in enumerate(plan):
            @pl.when(has & jnp.logical_not(local))
            def _():
                remote(block, dst, gsend.at[k, a], sem, to).wait_send()

    for k in range(2):
        @pl.when(u != 1 + 2 * k)
        def _():
            arrived(tb3.at[k], t3r.at[k])

    for t in range(STEPS):
        tr_ref[t] = tb3[0, t, 0] + tb3[1, t, 0]
    for a in range(ROWS):
        arrived(out_ref.at[a, 0], orecv.at[a, 0])

        @pl.when(u == a + ROWS)
        def _():
            arrived(out_ref.at[a, 1], orecv.at[a, 1])

        @pl.when(u != a + ROWS)
        def _():
            pltpu.make_async_copy(zero, out_ref.at[a, 1], zsem.at[a]).wait()


def solution(mesh):
    n_row, n_col, n_layer = (mesh.shape[name] for name in ("row", "col", "layer"))
    dma = pltpu.SemaphoreType.DMA

    def shards(blocks, columns, signs):
        def body(*refs):
            kernel(n_row, n_col, n_layer, *refs)

        f32, bf16 = jnp.float32, jnp.bfloat16
        return pl.pallas_call(
            body,
            out_shape=(jax.ShapeDtypeStruct(blocks.shape, f32), jax.ShapeDtypeStruct((STEPS,), f32)),
            in_specs=[
                pl.BlockSpec(memory_space=pltpu.SMEM),
                pl.BlockSpec(memory_space=pltpu.SMEM),
                pl.BlockSpec(memory_space=pltpu.HBM),
            ],
            out_specs=(pl.BlockSpec(memory_space=pl.ANY), pl.BlockSpec(memory_space=pltpu.SMEM)),
            scratch_shapes=[
                pltpu.VMEM((STEPS + 1, 10, B, B), f32),
                pltpu.VMEM((STEPS, 10, B, B), f32),
                pltpu.VMEM((STEPS, 10, B, B), f32),
                pltpu.VMEM((6 * B, 10 * B), bf16),
                pltpu.VMEM((6 * B, 10 * B), bf16),
                pltpu.VMEM((2, 2 * B, 2 * B), f32),
                pltpu.VMEM((10, B, B), f32),
                pltpu.VMEM((B, B), f32),
                pltpu.VMEM((8, B), f32),
                pltpu.VMEM((n_col, 8, B), f32),
                pltpu.VMEM((n_row, 8, B), f32),
                pltpu.VMEM((2, 8, B), f32),
                dma((4, ROWS)),
                dma((3, 10)),
                dma((STEPS, 6)),
                dma((STEPS, 6)),
                dma((2, 10)),
                dma((ROWS, 2)),
                dma((ROWS,)),
                dma((n_col,)),
                dma((n_col,)),
                dma((n_row,)),
                dma((n_row,)),
                dma((n_layer,)),
                dma((2,)),
            ],
            compiler_params=pltpu.CompilerParams(
                collective_id=0, has_side_effects=True, vmem_limit_bytes=60 * 1024 * 1024
            ),
        )(columns.T, signs, blocks)

    return jax.shard_map(
        shards,
        mesh=mesh,
        in_specs=(P(("row", "col"), "layer", None, None), P(), P()),
        out_specs=(P(("row", "col"), "layer", None, None), P()),
        check_vma=False,
    )
```

```python
import jax
import jax.numpy as jnp
from jax import lax
from jax.experimental import pallas as pl
from jax.experimental.pallas import tpu as pltpu
from jax.sharding import PartitionSpec as P

MESH = pl.DeviceIdType.MESH
B = 128
ROWS = 4
STEPS = 3
BLOCKS = ((0, 0), (0, 1), (1, 1), (0, 2), (0, 3), (1, 2), (1, 3), (-2, 2), (-1, 2), (-1, 3))
SPAN = {"A": (0, 3), "B": (3, 4), "D": (7, 3)}
CORNER = {"A": (0, 0), "B": (0, 2), "D": (-2, 2)}
UP, DOWN = 1, -1


def kernel(n_row, n_col, n_layer, cols_ref, signs_ref, blk_ref, out_ref, tr_ref, own, left, right, high, low, acc,
           flip, zero, mine, tb0, tb1, tb2, tb3, gsend, grecv, hsend, hrecv, osend, orecv, zsem, t0s, t0r, t1s, t1r, t2s, t2r,
           t3s, t3r):
    row, col, layer = lax.axis_index("row"), lax.axis_index("col"), lax.axis_index("layer")
    i32 = jnp.int32
    core = lax.rem(col, 2)
    base = 4 * core
    u = jnp.where(layer < base, layer - base + n_layer, layer - base)
    collector = (u == 1) | (u == 3)
    b = jnp.where(u == 3, 1, 0)
    first = (row == 0) & (col == 0)
    last = (row == n_row - 1) & (col == n_col - 1)
    wrap_up, wrap_down = col == n_col - 1, col == 0
    up = (jnp.where(wrap_up, jnp.where(row == n_row - 1, 0, row + 1), row), jnp.where(wrap_up, 0, col + 1))
    down = (jnp.where(wrap_down, jnp.where(row == 0, n_row - 1, row - 1), row), jnp.where(wrap_down, n_col - 1, col - 1))
    here = (row, col)
    far = 4 - base

    def pick(cond, x, y):
        return tuple(jnp.where(cond, p, q) for p, q in zip(x, y))

    peer = {
        1: pick(b == 0, (*here, base + 3), (*up, far + 1)),
        -1: pick(b == 0, (*down, far + 3), (*here, base + 1)),
    }
    slot_up = jnp.where(first, 0, 1)
    slot_up_before = jnp.where((row == 0) & (col == 1), 0, 1)
    slot_down = jnp.where(first, 1, 0)
    slot_down_after = jnp.where(last, 1, 0)

    def turn(x, p, n):
        return jnp.where(x + p >= n, x + p - n, x + p)

    def remote(src, dst, send, recv, to):
        return pltpu.make_async_remote_copy(src, dst, send, recv, device_id=to, device_id_type=MESH)

    def arrived(ref, sem):
        pltpu.make_async_copy(ref, ref, sem).wait()

    others = [(row, col, turn(layer, p, n_layer)) for p in range(1, n_layer)]
    adder = layer == 0
    col_peers = [(row, turn(col, p, n_col), layer) for p in range(1, n_col)]
    row_peers = [(turn(row, p, n_row), col, layer) for p in range(1, n_row)]

    barrier = pltpu.get_barrier_semaphore()

    def greet(to):
        pl.semaphore_signal(barrier, inc=1, device_id=to, device_id_type=MESH)

    def ready(group, start, columns):
        for k in columns:
            greet((*group, turn(start, k, n_layer)))

    @pl.when(u == 1)
    def _():
        ready(here, base, (0, 2, 3))
        ready(down, far, (2, 3, 4, 5, 6, 7))
        ready(up, far, (4, 5, 6, 7))

    @pl.when(u == 3)
    def _():
        ready(here, base, (0, 1, 2, 4, 5))
        ready(down, far, (6, 7))
        ready(up, far, (0, 1, 6, 7))

    for k in range(2):
        @pl.when(u != 1 + 2 * k)
        def _():
            greet((*here, base + 1 + 2 * k))

    greet((*down, far + 3))
    greet((*up, far + 1))

    @pl.when(jnp.logical_not(adder))
    def _():
        greet((*here, 0))

    @pl.when(collector)
    def _():
        for to in peer.values():
            greet(to)
        pl.semaphore_wait(barrier, 2 + (n_layer - 1) + n_layer + 2)

    @pl.when(adder)
    def _():
        for to in [*col_peers, *row_peers]:
            greet(to)
        pl.semaphore_wait(barrier, 3 + (n_layer - 1) + (n_col - 1) + (n_row - 1))

    @pl.when(jnp.logical_not(collector | adder) & (u < 6))
    def _():
        pl.semaphore_wait(barrier, 3)

    @pl.when(u >= 6)
    def _():
        pl.semaphore_wait(barrier, 4)

    def sources(a):
        pair, d, q = a // 2, u - a, u - 2 * (a // 2)
        two, four = jnp.where(q >= 2, 1, 0), jnp.where(q >= 4, 1, 0)
        n = q + 1 + 2 * two + four if a % 2 else q + two + 2 * four
        has = (d >= 0) & (d <= ROWS)
        block = blk_ref.at[a, jnp.where(d == ROWS, slot_up, 0)]
        mine_, next_ = (*here, base + 1 + 2 * pair), ((*here, base + 3) if a < 2 else (*up, far + 1))
        third = (*up, far + 1) if a < 2 else (*up, far + 3)
        yield has & (q < 2), block, right.at[0, n], grecv.at[2, n], (*down, far + 3) if a < 2 else (*here, base + 1), False
        yield has, block, left.at[0, n], grecv.at[1, n], pick(q >= 4, third, next_), u == 3 if a < 2 else False
        yield has, block, own.at[0, n], grecv.at[0, n], pick(q >= 4, next_, mine_), u == 1 + 2 * pair
        c = jnp.where(u < ROWS, u, u - n_layer) - 2 * pair + 2
        n = jnp.where(c >= 0, 3 + a % 2 + 2 * c, 9 + a % 2 + c)
        has = (u >= a + ROWS) | (u < 2) if a >= 2 else u >= a + ROWS
        block = blk_ref.at[a, jnp.where(u == a + ROWS, slot_down, 0)]
        yield has, block, right.at[0, n], grecv.at[2, n], (*down, far + 1 + 2 * pair), False

    plans = list(zip(*(sources(a) for a in range(ROWS))))
    for k, plan in enumerate(plans):
        for a, (has, block, dst, sem, to, local) in enumerate(plan):
            @pl.when(has & jnp.logical_not(local))
            def _():
                remote(block, dst, gsend.at[k, a], sem, to).start()

            if local is not False:
                @pl.when(has & local)
                def _():
                    pltpu.make_async_copy(block, dst, sem).start()

    zero[...] = jnp.zeros_like(zero)
    for a in range(ROWS):
        @pl.when(u != a + ROWS)
        def _():
            pltpu.make_async_copy(zero, out_ref.at[a, 1], zsem.at[a]).start()

    def copy(tile, way, t):
        part = pl.ds(*SPAN[tile])
        k = 2 * list(SPAN).index(tile) + (way == UP)
        dst = left if way == UP else right
        return remote(own.at[t, part], dst.at[t, part], hsend.at[t, k], hrecv.at[t, k], peer[way])

    def come(tile, way, t):
        part = pl.ds(*SPAN[tile])
        k = 2 * list(SPAN).index(tile) + (way == UP)
        dst = left if way == UP else right
        blocks = range(SPAN[tile][0], sum(SPAN[tile]))
        turned = way == DOWN and tile != "A"

        @pl.when(t == 0)
        def _():
            for n in blocks:
                arrived(dst.at[0, n], grecv.at[1 if way == UP else 2, n])
            if turned:
                for n in blocks:
                    a, q = BLOCKS[n]
                    put(a + 2, q + 2, dst[0, n].T)

        @pl.when(t > 0)
        def _():
            arrived(dst.at[t, part], hrecv.at[t, k])
            if turned:
                for n in blocks:
                    a, q = BLOCKS[n]
                    put(a + 2, q + 2, dst[t, n])

        if not turned:
            for n in blocks:
                a, q = BLOCKS[n]
                put_both(a - 2 * way, q - 2 * way, dst[t, n])

    def put(r, k, x):
        h = x.astype(jnp.bfloat16)
        lo = (x - h.astype(jnp.float32)).astype(jnp.bfloat16)
        high[(r + 2) * B:(r + 3) * B, (k + 4) * B:(k + 5) * B] = h
        low[(r + 2) * B:(r + 3) * B, (k + 4) * B:(k + 5) * B] = lo

    def put_both(r, k, x):
        if -2 <= r < 4:
            put(r, k, x)
        if k > r and -2 <= k < 4:
            put(k, r, x.T)

    def product(tile, start, stop):
        i, j = CORNER[tile]

        def part(ref, r):
            return ref[(r + 2) * B:(r + 4) * B, (start + 4) * B:(stop + 4) * B]

        def dot(x, y):
            return lax.dot_general(x, y, (((1,), (1,)), ((), ())), preferred_element_type=jnp.float32)

        ah, al, bh, bl = part(high, i), part(low, i), part(high, j), part(low, j)
        return dot(ah, bh) + (dot(al, bh) + dot(ah, bl))

    def there(a, q):
        at_row = ROWS * (row * n_col + col) + 2 * b + a
        at_col = at_row + q - a
        slot = 2 * turn(base + 2 * b, q, n_layer)
        r = jnp.maximum(at_row, 0)
        return (at_row >= 0) & ((cols_ref[slot, r] == at_col) | (cols_ref[slot + 1, r] == at_col))

    def finish(t, tile, total, masks):
        square = signs_ref[t] == 1
        keep = jnp.where(square, 0.0, 2.0).astype(jnp.float32)
        sign = jnp.where(square, 1.0, -1.0).astype(jnp.float32)
        start, size = SPAN[tile]
        for n in range(start, start + size):
            a, q = BLOCKS[n]
            factor = sign * masks[n]
            part = total[(a % 2) * B:(a % 2 + 1) * B, (q % 2) * B:(q % 2 + 1) * B]
            own[t + 1, n] = keep * own[t, n] + factor * part

    def results(tile):
        start, size = SPAN[tile]
        for n in range(start, start + size):
            a, q = BLOCKS[n]
            wide = q - a == ROWS
            at_a, at_q = turn(base + 2 * b, a % n_layer, n_layer), turn(base + 2 * b, q, n_layer)
            if a >= 0:
                group, r, slot = here, 2 * b + a, 0
            else:
                group = pick(b == 0, down, here)
                r = jnp.where(b == 0, ROWS + a, 2 + a)
                slot = jnp.where(b == 0, slot_up_before, slot_up) if wide else 0
            yield own.at[STEPS, n], out_ref.at[r, slot], osend.at[0, n], orecv.at[r, slot], (*group, at_q), q == 1
            if q > a:
                over = 2 * b + q >= ROWS
                group = pick(over, up, here)
                r = jnp.where(over, 2 * b + q - ROWS, 2 * b + q)
                slot = jnp.where(over, slot_down_after, slot_down) if wide else 0
                local = b == 0 if a == 1 else False
                yield flip.at[n], out_ref.at[r, slot], osend.at[1, n], orecv.at[r, slot], (*group, at_a), local

    def deliver(tile):
        start, size = SPAN[tile]
        for n in range(start, start + size):
            a, q = BLOCKS[n]
            if q > a:
                flip[n] = own[STEPS, n].T
        for src, dst, send, recv, to, local in results(tile):
            if local is not True:
                @pl.when(jnp.logical_not(local))
                def _():
                    remote(src, dst, send, recv, to).start()
            if local is not False:
                @pl.when(local)
                def _():
                    pltpu.make_async_copy(src, dst, recv).start()

    def delivered(tile):
        for src, dst, send, recv, to, local in results(tile):
            if local is not True:
                @pl.when(jnp.logical_not(local))
                def _():
                    remote(src, dst, send, recv, to).wait_send()

    def share():
        eye = lax.broadcasted_iota(i32, (B, B), 0) == lax.broadcasted_iota(i32, (B, B), 1)

        def diagonal(t):
            return jnp.sum(jnp.where(eye, own[t, 0] + own[t, 2], 0.0), axis=0, keepdims=True)

        one, two = diagonal(1), diagonal(2)
        diag = jnp.zeros((B, B), jnp.float32)
        off = jnp.zeros((B, B), jnp.float32)
        for n, (a, q) in enumerate(BLOCKS):
            x = own[2, n]
            if q > a:
                off = off + x * x
            else:
                diag = diag + x * x
        norm = jnp.sum(diag + 2.0 * off, axis=0, keepdims=True)
        three = jnp.where(signs_ref[2] == 1, norm, 2.0 * two - norm)
        line = lax.broadcasted_iota(i32, (8, B), 0)
        mine[...] = jnp.where(line == 0, one, jnp.where(line == 1, two, jnp.where(line == 2, three, 0.0)))
        remote(mine, tb0.at[b], t0s, t0r.at[b], (*here, 0)).start()

    @pl.when(adder)
    def _():
        for k in range(2):
            arrived(tb0.at[k], t0r.at[k])
        tb1[col] = tb0[0] + tb0[1]
        for p, to in enumerate(col_peers):
            remote(tb1.at[col], tb1.at[col], t1s.at[p], t1r.at[col], to).start()
        for p in range(1, n_col):
            c = turn(col, p, n_col)
            arrived(tb1.at[c], t1r.at[c])
        tb2[row] = jnp.sum(tb1[...], axis=0)
        for p, to in enumerate(row_peers):
            remote(tb2.at[row], tb2.at[row], t2s.at[p], t2r.at[row], to).start()
        for p in range(1, n_row):
            r = turn(row, p, n_row)
            arrived(tb2.at[r], t2r.at[r])
        total = jnp.sum(jnp.sum(tb2[...], axis=0), axis=1, keepdims=True) / (n_row * n_col * ROWS * B)
        mine[...] = jnp.broadcast_to(total, (8, B))
        for p, to in enumerate(others):
            remote(mine, tb3, t3s.at[p], t3r, to).start()
        tb3[...] = mine[...]
        for p, to in enumerate(col_peers):
            remote(tb1.at[col], tb1.at[col], t1s.at[p], t1r.at[col], to).wait_send()
        for p, to in enumerate(row_peers):
            remote(tb2.at[row], tb2.at[row], t2s.at[p], t2r.at[row], to).wait_send()
        for p, to in enumerate(others):
            remote(mine, tb3, t3s.at[p], t3r, to).wait_send()

    @pl.when(collector)
    def _():
        for r, k in ((0, 5), (1, -4), (3, -2), (-2, 3)):
            put(r, k, jnp.zeros((B, B), jnp.float32))
        masks = [jnp.where(there(a, q), 1.0, 0.0).astype(jnp.float32) for a, q in BLOCKS]

        for n in range(len(BLOCKS)):
            arrived(own.at[0, n], grecv.at[0, n])

        def step(t, carry):
            pl.when(t == 2)(share)
            for n, (a, q) in enumerate(BLOCKS):
                put_both(a, q, own[t, n])
            acc[0] = product("A", 0, 4)
            acc[1] = product("B", 0, 2)

            def send(when, *copies):
                @pl.when(when)
                def _():
                    for tile, way in copies:
                        copy(tile, way, t + 1).start()

            def make_d(even):
                come("A", DOWN, t)
                come("A", UP, t)
                finish(t, "D", product("D", -2, 4), masks)
                if even:
                    send(t == 0, ("D", UP), ("D", DOWN))
                    pl.when(t == 2)(lambda: deliver("D"))
                else:
                    copy("D", DOWN, 2).start()

            come("B", UP, t)
            pl.when(t != 1)(lambda: make_d(True))
            come("D", DOWN, t)
            come("D", UP, t)
            finish(t, "A", acc[0] + product("A", -4, 0) + product("A", 4, 6), masks)
            send(t < 2, ("A", DOWN))
            send(t == 1, ("A", UP))
            pl.when(t == 2)(lambda: deliver("A"))
            pl.when(t == 1)(lambda: make_d(False))
            come("B", DOWN, t)
            finish(t, "B", acc[1] + product("B", -2, 0) + product("B", 2, 6), masks)
            send(t < 2, ("B", UP), ("B", DOWN))
            send(t == 0, ("A", UP))
            send(t == 1, ("D", UP))

            pl.when(t == 2)(lambda: deliver("B"))
            return carry

        lax.fori_loop(0, STEPS, step, 0)

        for t in range(1, STEPS):
            for tile in SPAN:
                for way in (UP, DOWN):
                    copy(tile, way, t).wait_send()
        for tile in SPAN:
            delivered(tile)

        remote(mine, tb0.at[b], t0s, t0r.at[b], (*here, 0)).wait_send()

    for k, plan in enumerate(plans):
        for a, (has, block, dst, sem, to, local) in enumerate(plan):
            @pl.when(has & jnp.logical_not(local))
            def _():
                remote(block, dst, gsend.at[k, a], sem, to).wait_send()

    @pl.when(jnp.logical_not(adder))
    def _():
        arrived(tb3, t3r)

    for t in range(STEPS):
        tr_ref[t] = tb3[t, 0]
    for a in range(ROWS):
        arrived(out_ref.at[a, 0], orecv.at[a, 0])

        @pl.when(u == a + ROWS)
        def _():
            arrived(out_ref.at[a, 1], orecv.at[a, 1])

        @pl.when(u != a + ROWS)
        def _():
            pltpu.make_async_copy(zero, out_ref.at[a, 1], zsem.at[a]).wait()


def solution(mesh):
    n_row, n_col, n_layer = (mesh.shape[name] for name in ("row", "col", "layer"))
    dma = pltpu.SemaphoreType.DMA

    def shards(blocks, columns, signs):
        def body(*refs):
            kernel(n_row, n_col, n_layer, *refs)

        f32, bf16 = jnp.float32, jnp.bfloat16
        return pl.pallas_call(
            body,
            out_shape=(jax.ShapeDtypeStruct(blocks.shape, f32), jax.ShapeDtypeStruct((STEPS,), f32)),
            in_specs=[
                pl.BlockSpec(memory_space=pltpu.SMEM),
                pl.BlockSpec(memory_space=pltpu.SMEM),
                pl.BlockSpec(memory_space=pltpu.HBM),
            ],
            out_specs=(pl.BlockSpec(memory_space=pl.ANY), pl.BlockSpec(memory_space=pltpu.SMEM)),
            scratch_shapes=[
                pltpu.VMEM((STEPS + 1, 10, B, B), f32),
                pltpu.VMEM((STEPS, 10, B, B), f32),
                pltpu.VMEM((STEPS, 10, B, B), f32),
                pltpu.VMEM((6 * B, 10 * B), bf16),
                pltpu.VMEM((6 * B, 10 * B), bf16),
                pltpu.VMEM((2, 2 * B, 2 * B), f32),
                pltpu.VMEM((10, B, B), f32),
                pltpu.VMEM((B, B), f32),
                pltpu.VMEM((8, B), f32),
                pltpu.VMEM((2, 8, B), f32),
                pltpu.VMEM((n_col, 8, B), f32),
                pltpu.VMEM((n_row, 8, B), f32),
                pltpu.VMEM((8, B), f32),
                dma((4, ROWS)),
                dma((3, 10)),
                dma((STEPS, 6)),
                dma((STEPS, 6)),
                dma((2, 10)),
                dma((ROWS, 2)),
                dma((ROWS,)),
                dma,
                dma((2,)),
                dma((n_col,)),
                dma((n_col,)),
                dma((n_row,)),
                dma((n_row,)),
                dma((n_layer,)),
                dma,
            ],
            compiler_params=pltpu.CompilerParams(
                collective_id=0, has_side_effects=True, vmem_limit_bytes=60 * 1024 * 1024
            ),
        )(columns.T, signs, blocks)

    return jax.shard_map(
        shards,
        mesh=mesh,
        in_specs=(P(("row", "col"), "layer", None, None), P(), P()),
        out_specs=(P(("row", "col"), "layer", None, None), P()),
        check_vma=False,
    )
```

```python
import jax
import jax.numpy as jnp
from jax import lax
from jax.experimental import pallas as pl
from jax.experimental.pallas import tpu as pltpu
from jax.sharding import PartitionSpec as P

MESH = pl.DeviceIdType.MESH
B = 128
ROWS = 4
STEPS = 3
BLOCKS = ((0, 0), (0, 1), (1, 1), (0, 2), (0, 3), (1, 2), (1, 3), (-2, 2), (-1, 2), (-1, 3))
SPAN = {"A": (0, 3), "B": (3, 4), "D": (7, 3)}
CORNER = {"A": (0, 0), "B": (0, 2), "D": (-2, 2)}
UP, DOWN = 1, -1


def kernel(n_row, n_col, n_layer, cols_ref, signs_ref, blk_ref, out_ref, tr_ref, own, left, right, high, low, acc,
           flip, zero, mine, tb0, tb1, tb2, tb3, gsend, grecv, hsend, hrecv, osend, orecv, zsem, t0s, t0r, t1s, t1r, t2s, t2r,
           t3s, t3r):
    row, col, layer = lax.axis_index("row"), lax.axis_index("col"), lax.axis_index("layer")
    i32 = jnp.int32
    core = lax.rem(col, 2)
    base = 4 * core
    u = jnp.where(layer < base, layer - base + n_layer, layer - base)
    collector = (u == 1) | (u == 3)
    b = jnp.where(u == 3, 1, 0)
    first = (row == 0) & (col == 0)
    last = (row == n_row - 1) & (col == n_col - 1)
    wrap_up, wrap_down = col == n_col - 1, col == 0
    up = (jnp.where(wrap_up, jnp.where(row == n_row - 1, 0, row + 1), row), jnp.where(wrap_up, 0, col + 1))
    down = (jnp.where(wrap_down, jnp.where(row == 0, n_row - 1, row - 1), row), jnp.where(wrap_down, n_col - 1, col - 1))
    here = (row, col)
    far = 4 - base

    def pick(cond, x, y):
        return tuple(jnp.where(cond, p, q) for p, q in zip(x, y))

    peer = {
        1: pick(b == 0, (*here, base + 3), (*up, far + 1)),
        -1: pick(b == 0, (*down, far + 3), (*here, base + 1)),
    }
    slot_up = jnp.where(first, 0, 1)
    slot_up_before = jnp.where((row == 0) & (col == 1), 0, 1)
    slot_down = jnp.where(first, 1, 0)
    slot_down_after = jnp.where(last, 1, 0)

    def turn(x, p, n):
        return jnp.where(x + p >= n, x + p - n, x + p)

    def remote(src, dst, send, recv, to):
        return pltpu.make_async_remote_copy(src, dst, send, recv, device_id=to, device_id_type=MESH)

    def arrived(ref, sem):
        pltpu.make_async_copy(ref, ref, sem).wait()

    others = [(row, col, turn(layer, p, n_layer)) for p in range(1, n_layer)]
    adder = layer == 0
    col_peers = [(row, turn(col, p, n_col), layer) for p in range(1, n_col)]
    row_peers = [(turn(row, p, n_row), col, layer) for p in range(1, n_row)]

    barrier = pltpu.get_barrier_semaphore()

    def greet(to):
        pl.semaphore_signal(barrier, inc=1, device_id=to, device_id_type=MESH)

    def ready(group, start, columns):
        for k in columns:
            greet((*group, turn(start, k, n_layer)))

    @pl.when(u == 1)
    def _():
        ready(here, base, (0, 2, 3))
        ready(down, far, (2, 3, 4, 5, 6, 7))
        ready(up, far, (4, 5, 6, 7))

    @pl.when(u == 3)
    def _():
        ready(here, base, (0, 1, 2, 4, 5))
        ready(down, far, (6, 7))
        ready(up, far, (0, 1, 6, 7))

    for k in range(2):
        @pl.when(u != 1 + 2 * k)
        def _():
            greet((*here, base + 1 + 2 * k))

    greet((*down, far + 3))
    greet((*up, far + 1))

    @pl.when(jnp.logical_not(adder))
    def _():
        greet((*here, 0))

    @pl.when(collector)
    def _():
        for to in peer.values():
            greet(to)
        pl.semaphore_wait(barrier, 2 + (n_layer - 1) + n_layer + 2)

    @pl.when(adder)
    def _():
        for to in [*col_peers, *row_peers]:
            greet(to)
        pl.semaphore_wait(barrier, 3 + (n_layer - 1) + (n_col - 1) + (n_row - 1))

    @pl.when(jnp.logical_not(collector | adder) & (u < 6))
    def _():
        pl.semaphore_wait(barrier, 3)

    @pl.when(u >= 6)
    def _():
        pl.semaphore_wait(barrier, 4)

    def sources(a):
        pair, d, q = a // 2, u - a, u - 2 * (a // 2)
        two, four = jnp.where(q >= 2, 1, 0), jnp.where(q >= 4, 1, 0)
        n = q + 1 + 2 * two + four if a % 2 else q + two + 2 * four
        has = (d >= 0) & (d <= ROWS)
        block = blk_ref.at[a, jnp.where(d == ROWS, slot_up, 0)]
        mine_, next_ = (*here, base + 1 + 2 * pair), ((*here, base + 3) if a < 2 else (*up, far + 1))
        third = (*up, far + 1) if a < 2 else (*up, far + 3)
        yield has & (q < 2), block, right.at[0, n], grecv.at[2, n], (*down, far + 3) if a < 2 else (*here, base + 1), False
        yield has, block, left.at[0, n], grecv.at[1, n], pick(q >= 4, third, next_), u == 3 if a < 2 else False
        yield has, block, own.at[0, n], grecv.at[0, n], pick(q >= 4, next_, mine_), u == 1 + 2 * pair
        c = jnp.where(u < ROWS, u, u - n_layer) - 2 * pair + 2
        n = jnp.where(c >= 0, 3 + a % 2 + 2 * c, 9 + a % 2 + c)
        has = (u >= a + ROWS) | (u < 2) if a >= 2 else u >= a + ROWS
        block = blk_ref.at[a, jnp.where(u == a + ROWS, slot_down, 0)]
        yield has, block, right.at[0, n], grecv.at[2, n], (*down, far + 1 + 2 * pair), False

    plans = list(zip(*(sources(a) for a in range(ROWS))))
    for k, plan in enumerate(plans):
        for a, (has, block, dst, sem, to, local) in enumerate(plan):
            @pl.when(has & jnp.logical_not(local))
            def _():
                remote(block, dst, gsend.at[k, a], sem, to).start()

            if local is not False:
                @pl.when(has & local)
                def _():
                    pltpu.make_async_copy(block, dst, sem).start()

    zero[...] = jnp.zeros_like(zero)
    for a in range(ROWS):
        @pl.when(u != a + ROWS)
        def _():
            pltpu.make_async_copy(zero, out_ref.at[a, 1], zsem.at[a]).start()

    def copy(tile, way, t):
        part = pl.ds(*SPAN[tile])
        k = 2 * list(SPAN).index(tile) + (way == UP)
        dst = left if way == UP else right
        return remote(own.at[t, part], dst.at[t, part], hsend.at[t, k], hrecv.at[t, k], peer[way])

    def come(tile, way, t):
        part = pl.ds(*SPAN[tile])
        k = 2 * list(SPAN).index(tile) + (way == UP)
        dst = left if way == UP else right
        blocks = range(SPAN[tile][0], sum(SPAN[tile]))
        turned = way == DOWN and tile != "A"

        @pl.when(t == 0)
        def _():
            for n in blocks:
                arrived(dst.at[0, n], grecv.at[1 if way == UP else 2, n])
            if turned:
                for n in blocks:
                    a, q = BLOCKS[n]
                    put(a + 2, q + 2, dst[0, n].T)

        @pl.when(t > 0)
        def _():
            arrived(dst.at[t, part], hrecv.at[t, k])
            if turned:
                for n in blocks:
                    a, q = BLOCKS[n]
                    put(a + 2, q + 2, dst[t, n])

        if not turned:
            for n in blocks:
                a, q = BLOCKS[n]
                put_both(a - 2 * way, q - 2 * way, dst[t, n])

    def put(r, k, x):
        h = x.astype(jnp.bfloat16)
        lo = (x - h.astype(jnp.float32)).astype(jnp.bfloat16)
        high[(r + 2) * B:(r + 3) * B, (k + 4) * B:(k + 5) * B] = h
        low[(r + 2) * B:(r + 3) * B, (k + 4) * B:(k + 5) * B] = lo

    def put_both(r, k, x):
        if -2 <= r < 4:
            put(r, k, x)
        if k > r and -2 <= k < 4:
            put(k, r, x.T)

    def product(tile, start, stop):
        i, j = CORNER[tile]

        def part(ref, r):
            return ref[(r + 2) * B:(r + 4) * B, (start + 4) * B:(stop + 4) * B]

        def dot(x, y):
            return lax.dot_general(x, y, (((1,), (1,)), ((), ())), preferred_element_type=jnp.float32)

        ah, al, bh, bl = part(high, i), part(low, i), part(high, j), part(low, j)
        return dot(ah, bh) + (dot(al, bh) + dot(ah, bl))

    def there(a, q):
        at_row = ROWS * (row * n_col + col) + 2 * b + a
        at_col = at_row + q - a
        slot = 2 * turn(base + 2 * b, q, n_layer)
        r = jnp.maximum(at_row, 0)
        return (at_row >= 0) & ((cols_ref[slot, r] == at_col) | (cols_ref[slot + 1, r] == at_col))

    def finish(t, tile, total, masks):
        square = signs_ref[t] == 1
        keep = jnp.where(square, 0.0, 2.0).astype(jnp.float32)
        sign = jnp.where(square, 1.0, -1.0).astype(jnp.float32)
        start, size = SPAN[tile]
        for n in range(start, start + size):
            a, q = BLOCKS[n]
            factor = sign * masks[n]
            part = total[(a % 2) * B:(a % 2 + 1) * B, (q % 2) * B:(q % 2 + 1) * B]
            own[t + 1, n] = keep * own[t, n] + factor * part

    def results(tile):
        start, size = SPAN[tile]
        for n in range(start, start + size):
            a, q = BLOCKS[n]
            wide = q - a == ROWS
            at_a, at_q = turn(base + 2 * b, a % n_layer, n_layer), turn(base + 2 * b, q, n_layer)
            if a >= 0:
                group, r, slot = here, 2 * b + a, 0
            else:
                group = pick(b == 0, down, here)
                r = jnp.where(b == 0, ROWS + a, 2 + a)
                slot = jnp.where(b == 0, slot_up_before, slot_up) if wide else 0
            yield own.at[STEPS, n], out_ref.at[r, slot], osend.at[0, n], orecv.at[r, slot], (*group, at_q), q == 1
            if q > a:
                over = 2 * b + q >= ROWS
                group = pick(over, up, here)
                r = jnp.where(over, 2 * b + q - ROWS, 2 * b + q)
                slot = jnp.where(over, slot_down_after, slot_down) if wide else 0
                local = b == 0 if a == 1 else False
                yield flip.at[n], out_ref.at[r, slot], osend.at[1, n], orecv.at[r, slot], (*group, at_a), local

    def deliver(tile):
        start, size = SPAN[tile]
        for n in range(start, start + size):
            a, q = BLOCKS[n]
            if q > a:
                flip[n] = own[STEPS, n].T
        for src, dst, send, recv, to, local in results(tile):
            if local is not True:
                @pl.when(jnp.logical_not(local))
                def _():
                    remote(src, dst, send, recv, to).start()
            if local is not False:
                @pl.when(local)
                def _():
                    pltpu.make_async_copy(src, dst, recv).start()

    def delivered(tile):
        for src, dst, send, recv, to, local in results(tile):
            if local is not True:
                @pl.when(jnp.logical_not(local))
                def _():
                    remote(src, dst, send, recv, to).wait_send()

    def share():
        eye = lax.broadcasted_iota(i32, (B, B), 0) == lax.broadcasted_iota(i32, (B, B), 1)

        def diagonal(t):
            return jnp.sum(jnp.where(eye, own[t, 0] + own[t, 2], 0.0), axis=0, keepdims=True)

        one, two = diagonal(1), diagonal(2)
        diag = jnp.zeros((B, B), jnp.float32)
        off = jnp.zeros((B, B), jnp.float32)
        for n, (a, q) in enumerate(BLOCKS):
            x = own[2, n]
            if q > a:
                off = off + x * x
            else:
                diag = diag + x * x
        norm = jnp.sum(diag + 2.0 * off, axis=0, keepdims=True)
        three = jnp.where(signs_ref[2] == 1, norm, 2.0 * two - norm)
        line = lax.broadcasted_iota(i32, (8, B), 0)
        mine[...] = jnp.where(line == 0, one, jnp.where(line == 1, two, jnp.where(line == 2, three, 0.0)))
        remote(mine, tb0.at[b], t0s, t0r.at[b], (*here, 0)).start()

    @pl.when(adder)
    def _():
        for k in range(2):
            arrived(tb0.at[k], t0r.at[k])
        tb1[col] = tb0[0] + tb0[1]
        for p, to in enumerate(col_peers):
            remote(tb1.at[col], tb1.at[col], t1s.at[p], t1r.at[col], to).start()
        for p in range(1, n_col):
            c = turn(col, p, n_col)
            arrived(tb1.at[c], t1r.at[c])
        tb2[row] = jnp.sum(tb1[...], axis=0)
        for p, to in enumerate(row_peers):
            remote(tb2.at[row], tb2.at[row], t2s.at[p], t2r.at[row], to).start()
        for p in range(1, n_row):
            r = turn(row, p, n_row)
            arrived(tb2.at[r], t2r.at[r])
        total = jnp.sum(jnp.sum(tb2[...], axis=0), axis=1, keepdims=True) / (n_row * n_col * ROWS * B)
        mine[...] = jnp.broadcast_to(total, (8, B))
        for p, to in enumerate(others):
            remote(mine, tb3, t3s.at[p], t3r, to).start()
        tb3[...] = mine[...]
        for p, to in enumerate(col_peers):
            remote(tb1.at[col], tb1.at[col], t1s.at[p], t1r.at[col], to).wait_send()
        for p, to in enumerate(row_peers):
            remote(tb2.at[row], tb2.at[row], t2s.at[p], t2r.at[row], to).wait_send()
        for p, to in enumerate(others):
            remote(mine, tb3, t3s.at[p], t3r, to).wait_send()

    @pl.when(collector)
    def _():
        for r, k in ((0, 5), (1, -4), (3, -2), (-2, 3)):
            put(r, k, jnp.zeros((B, B), jnp.float32))
        masks = [jnp.where(there(a, q), 1.0, 0.0).astype(jnp.float32) for a, q in BLOCKS]

        for n in range(len(BLOCKS)):
            arrived(own.at[0, n], grecv.at[0, n])

        def step(t, carry):
            pl.when(t == 2)(share)
            for n, (a, q) in enumerate(BLOCKS):
                put_both(a, q, own[t, n])
            acc[0] = product("A", 0, 4)
            acc[1] = product("B", 0, 2)

            def send(when, *copies):
                @pl.when(when)
                def _():
                    for tile, way in copies:
                        copy(tile, way, t + 1).start()

            def make_d(even):
                come("A", DOWN, t)
                come("A", UP, t)
                finish(t, "D", product("D", -2, 4), masks)
                if even:
                    send(t == 0, ("D", UP), ("D", DOWN))
                    pl.when(t == 2)(lambda: deliver("D"))
                else:
                    copy("D", DOWN, 2).start()

            come("B", UP, t)
            pl.when(t != 1)(lambda: make_d(True))
            def make_a():
                finish(t, "A", acc[0] + product("A", -4, 0) + product("A", 4, 6), masks)

            def make_b():
                come("B", DOWN, t)
                finish(t, "B", acc[1] + product("B", -2, 0) + product("B", 2, 6), masks)

            come("D", DOWN, t)

            @pl.when(t < 2)
            def _():
                come("D", UP, t)
                make_a()
                copy("A", DOWN, t + 1).start()
                send(t == 1, ("A", UP))
                pl.when(t == 1)(lambda: make_d(False))
                make_b()
                copy("B", UP, t + 1).start()
                copy("B", DOWN, t + 1).start()
                send(t == 0, ("A", UP))
                send(t == 1, ("D", UP))

            @pl.when(t == 2)
            def _():
                make_b()
                deliver("B")
                come("D", UP, t)
                make_a()
                deliver("A")

            return carry

        lax.fori_loop(0, STEPS, step, 0)

        for t in range(1, STEPS):
            for tile in SPAN:
                for way in (UP, DOWN):
                    copy(tile, way, t).wait_send()
        for tile in SPAN:
            delivered(tile)

        remote(mine, tb0.at[b], t0s, t0r.at[b], (*here, 0)).wait_send()

    for k, plan in enumerate(plans):
        for a, (has, block, dst, sem, to, local) in enumerate(plan):
            @pl.when(has & jnp.logical_not(local))
            def _():
                remote(block, dst, gsend.at[k, a], sem, to).wait_send()

    @pl.when(jnp.logical_not(adder))
    def _():
        arrived(tb3, t3r)

    for t in range(STEPS):
        tr_ref[t] = tb3[t, 0]
    for a in range(ROWS):
        arrived(out_ref.at[a, 0], orecv.at[a, 0])

        @pl.when(u == a + ROWS)
        def _():
            arrived(out_ref.at[a, 1], orecv.at[a, 1])

        @pl.when(u != a + ROWS)
        def _():
            pltpu.make_async_copy(zero, out_ref.at[a, 1], zsem.at[a]).wait()


def hand_over(out_ref, tr_ref, result_ref, traces_ref):
    result_ref[...] = out_ref[...]
    for t in range(STEPS):
        traces_ref[t] = tr_ref[t]


def solution(mesh):
    n_row, n_col, n_layer = (mesh.shape[name] for name in ("row", "col", "layer"))
    dma = pltpu.SemaphoreType.DMA

    def shards(blocks, columns, signs):
        def body(*refs):
            kernel(n_row, n_col, n_layer, *refs)

        f32, bf16 = jnp.float32, jnp.bfloat16
        out, traces = pl.pallas_call(
            body,
            out_shape=(jax.ShapeDtypeStruct(blocks.shape, f32), jax.ShapeDtypeStruct((STEPS,), f32)),
            in_specs=[
                pl.BlockSpec(memory_space=pltpu.SMEM),
                pl.BlockSpec(memory_space=pltpu.SMEM),
                pl.BlockSpec(memory_space=pltpu.HBM),
            ],
            out_specs=(pl.BlockSpec(memory_space=pl.ANY), pl.BlockSpec(memory_space=pltpu.SMEM)),
            scratch_shapes=[
                pltpu.VMEM((STEPS + 1, 10, B, B), f32),
                pltpu.VMEM((STEPS, 10, B, B), f32),
                pltpu.VMEM((STEPS, 10, B, B), f32),
                pltpu.VMEM((6 * B, 10 * B), bf16),
                pltpu.VMEM((6 * B, 10 * B), bf16),
                pltpu.VMEM((2, 2 * B, 2 * B), f32),
                pltpu.VMEM((10, B, B), f32),
                pltpu.VMEM((B, B), f32),
                pltpu.VMEM((8, B), f32),
                pltpu.VMEM((2, 8, B), f32),
                pltpu.VMEM((n_col, 8, B), f32),
                pltpu.VMEM((n_row, 8, B), f32),
                pltpu.VMEM((8, B), f32),
                dma((4, ROWS)),
                dma((3, 10)),
                dma((STEPS, 6)),
                dma((STEPS, 6)),
                dma((2, 10)),
                dma((ROWS, 2)),
                dma((ROWS,)),
                dma,
                dma((2,)),
                dma((n_col,)),
                dma((n_col,)),
                dma((n_row,)),
                dma((n_row,)),
                dma((n_layer,)),
                dma,
            ],
            compiler_params=pltpu.CompilerParams(
                collective_id=0, has_side_effects=True, vmem_limit_bytes=60 * 1024 * 1024
            ),
        )(columns.T, signs, blocks)
        half = pl.BlockSpec((ROWS // 2, 2, B, B), lambda i: (i, 0, 0, 0))
        return pl.pallas_call(
            hand_over,
            grid=(2,),
            out_shape=(jax.ShapeDtypeStruct(blocks.shape, f32), jax.ShapeDtypeStruct((STEPS,), f32)),
            in_specs=[half, pl.BlockSpec(memory_space=pltpu.SMEM)],
            out_specs=(half, pl.BlockSpec(memory_space=pltpu.SMEM)),
            compiler_params=pltpu.CompilerParams(vmem_limit_bytes=60 * 1024 * 1024),
        )(out, traces)

    return jax.shard_map(
        shards,
        mesh=mesh,
        in_specs=(P(("row", "col"), "layer", None, None), P(), P()),
        out_specs=(P(("row", "col"), "layer", None, None), P()),
        check_vma=False,
    )
```

```python
import jax
import jax.numpy as jnp
from jax import lax
from jax.experimental import pallas as pl
from jax.experimental.pallas import tpu as pltpu
from jax.sharding import PartitionSpec as P

MESH = pl.DeviceIdType.MESH
B = 128
ROWS = 4
STEPS = 3
BLOCKS = ((0, 0), (0, 1), (1, 1), (0, 2), (0, 3), (1, 2), (1, 3), (-2, 2), (-1, 2), (-1, 3))
SPAN = {"A": (0, 3), "B": (3, 4), "D": (7, 3)}
CORNER = {"A": (0, 0), "B": (0, 2), "D": (-2, 2)}
UP, DOWN = 1, -1


def kernel(n_row, n_col, n_layer, cols_ref, signs_ref, blk_ref, out_ref, tr_ref, own, left, right, split, acc_a, acc_b,
           flip, zero, mine, tb0, tb1, tb2, tb3, gsend, grecv, hsend, hrecv, osend, orecv, zsem, t0s, t0r, t1s, t1r, t2s, t2r,
           t3s, t3r):
    row, col, layer = lax.axis_index("row"), lax.axis_index("col"), lax.axis_index("layer")
    i32 = jnp.int32
    core = lax.rem(col, 2)
    base = 4 * core
    u = jnp.where(layer < base, layer - base + n_layer, layer - base)
    collector = (u == 1) | (u == 3)
    b = jnp.where(u == 3, 1, 0)
    first = (row == 0) & (col == 0)
    last = (row == n_row - 1) & (col == n_col - 1)
    wrap_up, wrap_down = col == n_col - 1, col == 0
    up = (jnp.where(wrap_up, jnp.where(row == n_row - 1, 0, row + 1), row), jnp.where(wrap_up, 0, col + 1))
    down = (jnp.where(wrap_down, jnp.where(row == 0, n_row - 1, row - 1), row), jnp.where(wrap_down, n_col - 1, col - 1))
    here = (row, col)
    far = 4 - base

    def pick(cond, x, y):
        return tuple(jnp.where(cond, p, q) for p, q in zip(x, y))

    peer = {
        1: pick(b == 0, (*here, base + 3), (*up, far + 1)),
        -1: pick(b == 0, (*down, far + 3), (*here, base + 1)),
    }
    slot_up = jnp.where(first, 0, 1)
    slot_up_before = jnp.where((row == 0) & (col == 1), 0, 1)
    slot_down = jnp.where(first, 1, 0)
    slot_down_after = jnp.where(last, 1, 0)

    def turn(x, p, n):
        return jnp.where(x + p >= n, x + p - n, x + p)

    def remote(src, dst, send, recv, to):
        return pltpu.make_async_remote_copy(src, dst, send, recv, device_id=to, device_id_type=MESH)

    def arrived(ref, sem):
        pltpu.make_async_copy(ref, ref, sem).wait()

    others = [(row, col, turn(layer, p, n_layer)) for p in range(1, n_layer)]
    adder = layer == 0
    col_peers = [(row, turn(col, p, n_col), layer) for p in range(1, n_col)]
    row_peers = [(turn(row, p, n_row), col, layer) for p in range(1, n_row)]

    barrier = pltpu.get_barrier_semaphore()

    def greet(to):
        pl.semaphore_signal(barrier, inc=1, device_id=to, device_id_type=MESH)

    def ready(group, start, columns):
        for k in columns:
            greet((*group, turn(start, k, n_layer)))

    @pl.when(u == 1)
    def _():
        ready(here, base, (0, 2, 3))
        ready(down, far, (2, 3, 4, 5, 6, 7))
        ready(up, far, (4, 5, 6, 7))

    @pl.when(u == 3)
    def _():
        ready(here, base, (0, 1, 2, 4, 5))
        ready(down, far, (6, 7))
        ready(up, far, (0, 1, 6, 7))

    for k in range(2):
        @pl.when(u != 1 + 2 * k)
        def _():
            greet((*here, base + 1 + 2 * k))

    greet((*down, far + 3))
    greet((*up, far + 1))

    @pl.when(jnp.logical_not(adder))
    def _():
        greet((*here, 0))

    @pl.when(collector)
    def _():
        for to in peer.values():
            greet(to)
        pl.semaphore_wait(barrier, 2 + (n_layer - 1) + n_layer + 2)

    @pl.when(adder)
    def _():
        for to in [*col_peers, *row_peers]:
            greet(to)
        pl.semaphore_wait(barrier, 3 + (n_layer - 1) + (n_col - 1) + (n_row - 1))

    @pl.when(jnp.logical_not(collector | adder) & (u < 6))
    def _():
        pl.semaphore_wait(barrier, 3)

    @pl.when(u >= 6)
    def _():
        pl.semaphore_wait(barrier, 4)

    def sources(a):
        pair, d, q = a // 2, u - a, u - 2 * (a // 2)
        two, four = jnp.where(q >= 2, 1, 0), jnp.where(q >= 4, 1, 0)
        n = q + 1 + 2 * two + four if a % 2 else q + two + 2 * four
        has = (d >= 0) & (d <= ROWS)
        block = blk_ref.at[a, jnp.where(d == ROWS, slot_up, 0)]
        mine_, next_ = (*here, base + 1 + 2 * pair), ((*here, base + 3) if a < 2 else (*up, far + 1))
        third = (*up, far + 1) if a < 2 else (*up, far + 3)
        yield has & (q < 2), block, right.at[0, n], grecv.at[2, n], (*down, far + 3) if a < 2 else (*here, base + 1), False
        yield has, block, left.at[0, n], grecv.at[1, n], pick(q >= 4, third, next_), u == 3 if a < 2 else False
        yield has, block, own.at[0, n], grecv.at[0, n], pick(q >= 4, next_, mine_), u == 1 + 2 * pair
        c = jnp.where(u < ROWS, u, u - n_layer) - 2 * pair + 2
        n = jnp.where(c >= 0, 3 + a % 2 + 2 * c, 9 + a % 2 + c)
        has = (u >= a + ROWS) | (u < 2) if a >= 2 else u >= a + ROWS
        block = blk_ref.at[a, jnp.where(u == a + ROWS, slot_down, 0)]
        yield has, block, right.at[0, n], grecv.at[2, n], (*down, far + 1 + 2 * pair), False

    plans = list(zip(*(sources(a) for a in range(ROWS))))
    for k, plan in enumerate(plans):
        for a, (has, block, dst, sem, to, local) in enumerate(plan):
            @pl.when(has & jnp.logical_not(local))
            def _():
                remote(block, dst, gsend.at[k, a], sem, to).start()

            if local is not False:
                @pl.when(has & local)
                def _():
                    pltpu.make_async_copy(block, dst, sem).start()

    zero[...] = jnp.zeros_like(zero)
    for a in range(ROWS):
        @pl.when(u != a + ROWS)
        def _():
            pltpu.make_async_copy(zero, out_ref.at[a, 1], zsem.at[a]).start()

    def copy(tile, way, t):
        part = pl.ds(*SPAN[tile])
        k = 2 * list(SPAN).index(tile) + (way == UP)
        dst = left if way == UP else right
        return remote(own.at[t, part], dst.at[t, part], hsend.at[t, k], hrecv.at[t, k], peer[way])

    def come(tile, way, t):
        part = pl.ds(*SPAN[tile])
        k = 2 * list(SPAN).index(tile) + (way == UP)
        dst = left if way == UP else right
        blocks = range(SPAN[tile][0], sum(SPAN[tile]))
        turned = way == DOWN and tile != "A"

        @pl.when(t == 0)
        def _():
            for n in blocks:
                arrived(dst.at[0, n], grecv.at[1 if way == UP else 2, n])
            if turned:
                for n in blocks:
                    a, q = BLOCKS[n]
                    put(a + 2, q + 2, dst[0, n].T)

        @pl.when(t > 0)
        def _():
            arrived(dst.at[t, part], hrecv.at[t, k])
            if turned:
                for n in blocks:
                    a, q = BLOCKS[n]
                    put(a + 2, q + 2, dst[t, n])

        if not turned:
            for n in blocks:
                a, q = BLOCKS[n]
                put_both(a - 2 * way, q - 2 * way, dst[t, n])

    def put(r, k, x):
        h = x.astype(jnp.bfloat16)
        at = ((r + 2) // 2 * 4 + r % 2) * B
        split[at:at + B, (k + 4) * B:(k + 5) * B] = h
        split[at + 2 * B:at + 3 * B, (k + 4) * B:(k + 5) * B] = (x - h.astype(jnp.float32)).astype(jnp.bfloat16)

    def put_both(r, k, x):
        if -2 <= r < 4:
            put(r, k, x)
        if k > r and -2 <= k < 4:
            put(k, r, x.T)

    def product(tile, start, stop):
        i, j = CORNER[tile]

        def part(r, first, last):
            at = (r + 2) * 2 * B
            return split[at + first * B:at + last * B, (start + 4) * B:(stop + 4) * B]

        def dot(x, y):
            return lax.dot_general(x, y, (((1,), (1,)), ((), ())), preferred_element_type=jnp.float32)

        both = dot(part(i, 0, 4), part(j, 0, 2))
        if tile == "A":
            return both
        return both[:2 * B] + (both[2 * B:] + dot(part(i, 0, 2), part(j, 2, 4)))

    def whole(both):
        return both[:2 * B] + (both[2 * B:] + both[2 * B:].T)

    def there(a, q):
        at_row = ROWS * (row * n_col + col) + 2 * b + a
        at_col = at_row + q - a
        slot = 2 * turn(base + 2 * b, q, n_layer)
        r = jnp.maximum(at_row, 0)
        return (at_row >= 0) & ((cols_ref[slot, r] == at_col) | (cols_ref[slot + 1, r] == at_col))

    def finish(t, tile, total, masks):
        square = signs_ref[t] == 1
        keep = jnp.where(square, 0.0, 2.0).astype(jnp.float32)
        sign = jnp.where(square, 1.0, -1.0).astype(jnp.float32)
        start, size = SPAN[tile]
        for n in range(start, start + size):
            a, q = BLOCKS[n]
            factor = sign * masks[n]
            part = total[(a % 2) * B:(a % 2 + 1) * B, (q % 2) * B:(q % 2 + 1) * B]
            own[t + 1, n] = keep * own[t, n] + factor * part

    def results(tile):
        start, size = SPAN[tile]
        for n in range(start, start + size):
            a, q = BLOCKS[n]
            wide = q - a == ROWS
            at_a, at_q = turn(base + 2 * b, a % n_layer, n_layer), turn(base + 2 * b, q, n_layer)
            if a >= 0:
                group, r, slot = here, 2 * b + a, 0
            else:
                group = pick(b == 0, down, here)
                r = jnp.where(b == 0, ROWS + a, 2 + a)
                slot = jnp.where(b == 0, slot_up_before, slot_up) if wide else 0
            yield own.at[STEPS, n], out_ref.at[r, slot], osend.at[0, n], orecv.at[r, slot], (*group, at_q), q == 1
            if q > a:
                over = 2 * b + q >= ROWS
                group = pick(over, up, here)
                r = jnp.where(over, 2 * b + q - ROWS, 2 * b + q)
                slot = jnp.where(over, slot_down_after, slot_down) if wide else 0
                local = b == 0 if a == 1 else False
                yield flip.at[n], out_ref.at[r, slot], osend.at[1, n], orecv.at[r, slot], (*group, at_a), local

    def deliver(tile):
        start, size = SPAN[tile]
        for n in range(start, start + size):
            a, q = BLOCKS[n]
            if q > a:
                flip[n] = own[STEPS, n].T
        for src, dst, send, recv, to, local in results(tile):
            if local is not True:
                @pl.when(jnp.logical_not(local))
                def _():
                    remote(src, dst, send, recv, to).start()
            if local is not False:
                @pl.when(local)
                def _():
                    pltpu.make_async_copy(src, dst, recv).start()

    def delivered(tile):
        for src, dst, send, recv, to, local in results(tile):
            if local is not True:
                @pl.when(jnp.logical_not(local))
                def _():
                    remote(src, dst, send, recv, to).wait_send()

    def share():
        eye = lax.broadcasted_iota(i32, (B, B), 0) == lax.broadcasted_iota(i32, (B, B), 1)

        def diagonal(t):
            return jnp.sum(jnp.where(eye, own[t, 0] + own[t, 2], 0.0), axis=0, keepdims=True)

        one, two = diagonal(1), diagonal(2)
        diag = jnp.zeros((B, B), jnp.float32)
        off = jnp.zeros((B, B), jnp.float32)
        for n, (a, q) in enumerate(BLOCKS):
            x = own[2, n]
            if q > a:
                off = off + x * x
            else:
                diag = diag + x * x
        norm = jnp.sum(diag + 2.0 * off, axis=0, keepdims=True)
        three = jnp.where(signs_ref[2] == 1, norm, 2.0 * two - norm)
        line = lax.broadcasted_iota(i32, (8, B), 0)
        mine[...] = jnp.where(line == 0, one, jnp.where(line == 1, two, jnp.where(line == 2, three, 0.0)))
        remote(mine, tb0.at[b], t0s, t0r.at[b], (*here, 0)).start()

    @pl.when(adder)
    def _():
        for k in range(2):
            arrived(tb0.at[k], t0r.at[k])
        tb1[col] = tb0[0] + tb0[1]
        for p, to in enumerate(col_peers):
            remote(tb1.at[col], tb1.at[col], t1s.at[p], t1r.at[col], to).start()
        for p in range(1, n_col):
            c = turn(col, p, n_col)
            arrived(tb1.at[c], t1r.at[c])
        tb2[row] = jnp.sum(tb1[...], axis=0)
        for p, to in enumerate(row_peers):
            remote(tb2.at[row], tb2.at[row], t2s.at[p], t2r.at[row], to).start()
        for p in range(1, n_row):
            r = turn(row, p, n_row)
            arrived(tb2.at[r], t2r.at[r])
        total = jnp.sum(jnp.sum(tb2[...], axis=0), axis=1, keepdims=True) / (n_row * n_col * ROWS * B)
        mine[...] = jnp.broadcast_to(total, (8, B))
        for p, to in enumerate(others):
            remote(mine, tb3, t3s.at[p], t3r, to).start()
        tb3[...] = mine[...]
        for p, to in enumerate(col_peers):
            remote(tb1.at[col], tb1.at[col], t1s.at[p], t1r.at[col], to).wait_send()
        for p, to in enumerate(row_peers):
            remote(tb2.at[row], tb2.at[row], t2s.at[p], t2r.at[row], to).wait_send()
        for p, to in enumerate(others):
            remote(mine, tb3, t3s.at[p], t3r, to).wait_send()

    @pl.when(collector)
    def _():
        for r, k in ((0, 5), (1, -4), (3, -2), (-2, 3)):
            put(r, k, jnp.zeros((B, B), jnp.float32))
        masks = [jnp.where(there(a, q), 1.0, 0.0).astype(jnp.float32) for a, q in BLOCKS]

        for n in range(len(BLOCKS)):
            arrived(own.at[0, n], grecv.at[0, n])

        def step(t, carry):
            pl.when(t == 2)(share)
            for n, (a, q) in enumerate(BLOCKS):
                put_both(a, q, own[t, n])
            def within():
                acc_a[...] = product("A", 0, 4)
                acc_b[...] = product("B", 0, 2)

            pl.when(t > 0)(within)

            def send(when, *copies):
                @pl.when(when)
                def _():
                    for tile, way in copies:
                        copy(tile, way, t + 1).start()

            def make_d(even):
                come("A", DOWN, t)
                come("A", UP, t)
                finish(t, "D", product("D", -2, 4), masks)
                if even:
                    send(t == 0, ("D", UP), ("D", DOWN))
                    pl.when(t == 2)(lambda: deliver("D"))
                else:
                    copy("D", DOWN, 2).start()

            come("B", UP, t)
            pl.when(t != 1)(lambda: make_d(True))
            pl.when(t == 0)(within)
            def make_a():
                finish(t, "A", whole(acc_a[...] + product("A", -4, 0) + product("A", 4, 6)), masks)

            def make_b():
                come("B", DOWN, t)
                finish(t, "B", acc_b[...] + product("B", -2, 0) + product("B", 2, 6), masks)

            come("D", DOWN, t)

            @pl.when(t < 2)
            def _():
                come("D", UP, t)
                make_a()
                copy("A", DOWN, t + 1).start()
                send(t == 1, ("A", UP))
                pl.when(t == 1)(lambda: make_d(False))
                make_b()
                copy("B", UP, t + 1).start()
                copy("B", DOWN, t + 1).start()
                send(t == 0, ("A", UP))
                send(t == 1, ("D", UP))

            @pl.when(t == 2)
            def _():
                make_b()
                deliver("B")
                come("D", UP, t)
                make_a()
                deliver("A")

            return carry

        lax.fori_loop(0, STEPS, step, 0)

        for t in range(1, STEPS):
            for tile in SPAN:
                for way in (UP, DOWN):
                    copy(tile, way, t).wait_send()
        for tile in SPAN:
            delivered(tile)

        remote(mine, tb0.at[b], t0s, t0r.at[b], (*here, 0)).wait_send()

    for k, plan in enumerate(plans):
        for a, (has, block, dst, sem, to, local) in enumerate(plan):
            @pl.when(has & jnp.logical_not(local))
            def _():
                remote(block, dst, gsend.at[k, a], sem, to).wait_send()

    @pl.when(jnp.logical_not(adder))
    def _():
        arrived(tb3, t3r)

    for t in range(STEPS):
        tr_ref[t] = tb3[t, 0]
    for a in range(ROWS):
        arrived(out_ref.at[a, 0], orecv.at[a, 0])

        @pl.when(u == a + ROWS)
        def _():
            arrived(out_ref.at[a, 1], orecv.at[a, 1])

        @pl.when(u != a + ROWS)
        def _():
            pltpu.make_async_copy(zero, out_ref.at[a, 1], zsem.at[a]).wait()


def hand_over(out_ref, tr_ref, result_ref, traces_ref):
    result_ref[...] = out_ref[...]
    for t in range(STEPS):
        traces_ref[t] = tr_ref[t]


def solution(mesh):
    n_row, n_col, n_layer = (mesh.shape[name] for name in ("row", "col", "layer"))
    dma = pltpu.SemaphoreType.DMA

    def shards(blocks, columns, signs):
        def body(*refs):
            kernel(n_row, n_col, n_layer, *refs)

        f32, bf16 = jnp.float32, jnp.bfloat16
        out, traces = pl.pallas_call(
            body,
            out_shape=(jax.ShapeDtypeStruct(blocks.shape, f32), jax.ShapeDtypeStruct((STEPS,), f32)),
            in_specs=[
                pl.BlockSpec(memory_space=pltpu.SMEM),
                pl.BlockSpec(memory_space=pltpu.SMEM),
                pl.BlockSpec(memory_space=pltpu.HBM),
            ],
            out_specs=(pl.BlockSpec(memory_space=pl.ANY), pl.BlockSpec(memory_space=pltpu.SMEM)),
            scratch_shapes=[
                pltpu.VMEM((STEPS + 1, 10, B, B), f32),
                pltpu.VMEM((STEPS, 10, B, B), f32),
                pltpu.VMEM((STEPS, 10, B, B), f32),
                pltpu.VMEM((12 * B, 10 * B), bf16),
                pltpu.VMEM((4 * B, 2 * B), f32),
                pltpu.VMEM((2 * B, 2 * B), f32),
                pltpu.VMEM((10, B, B), f32),
                pltpu.VMEM((B, B), f32),
                pltpu.VMEM((8, B), f32),
                pltpu.VMEM((2, 8, B), f32),
                pltpu.VMEM((n_col, 8, B), f32),
                pltpu.VMEM((n_row, 8, B), f32),
                pltpu.VMEM((8, B), f32),
                dma((4, ROWS)),
                dma((3, 10)),
                dma((STEPS, 6)),
                dma((STEPS, 6)),
                dma((2, 10)),
                dma((ROWS, 2)),
                dma((ROWS,)),
                dma,
                dma((2,)),
                dma((n_col,)),
                dma((n_col,)),
                dma((n_row,)),
                dma((n_row,)),
                dma((n_layer,)),
                dma,
            ],
            compiler_params=pltpu.CompilerParams(
                collective_id=0, has_side_effects=True, vmem_limit_bytes=60 * 1024 * 1024
            ),
        )(columns.T, signs, blocks)
        half = pl.BlockSpec((ROWS // 2, 2, B, B), lambda i: (i, 0, 0, 0))
        return pl.pallas_call(
            hand_over,
            grid=(2,),
            out_shape=(jax.ShapeDtypeStruct(blocks.shape, f32), jax.ShapeDtypeStruct((STEPS,), f32)),
            in_specs=[half, pl.BlockSpec(memory_space=pltpu.SMEM)],
            out_specs=(half, pl.BlockSpec(memory_space=pltpu.SMEM)),
            compiler_params=pltpu.CompilerParams(vmem_limit_bytes=60 * 1024 * 1024),
        )(out, traces)

    return jax.shard_map(
        shards,
        mesh=mesh,
        in_specs=(P(("row", "col"), "layer", None, None), P(), P()),
        out_specs=(P(("row", "col"), "layer", None, None), P()),
        check_vma=False,
    )
```

```python
import jax
import jax.numpy as jnp
from jax import lax
from jax.experimental import pallas as pl
from jax.experimental.pallas import tpu as pltpu
from jax.sharding import PartitionSpec as P

MESH = pl.DeviceIdType.MESH
B = 128
ROWS = 4
STEPS = 3
BLOCKS = ((0, 0), (0, 1), (1, 1), (0, 2), (0, 3), (1, 2), (1, 3), (-2, 2), (-1, 2), (-1, 3))
SPAN = {"A": (0, 3), "B": (3, 4), "D": (7, 3)}
CORNER = {"A": (0, 0), "B": (0, 2), "D": (-2, 2)}
UP, DOWN = 1, -1


def kernel(n_row, n_col, n_layer, cols_ref, signs_ref, blk_ref, out_ref, tr_ref, own, left, right, split, acc_a, acc_b,
           flip, zero, mine, tb0, tb1, tb2, tb3, gsend, grecv, hsend, hrecv, osend, orecv, zsem, t0s, t0r, t1s, t1r, t2s, t2r,
           t3s, t3r):
    row, col, layer = lax.axis_index("row"), lax.axis_index("col"), lax.axis_index("layer")
    i32 = jnp.int32
    core = lax.rem(col, 2)
    base = 4 * core
    u = jnp.where(layer < base, layer - base + n_layer, layer - base)
    collector = (u == 1) | (u == 3)
    b = jnp.where(u == 3, 1, 0)
    first = (row == 0) & (col == 0)
    last = (row == n_row - 1) & (col == n_col - 1)
    wrap_up, wrap_down = col == n_col - 1, col == 0
    up = (jnp.where(wrap_up, jnp.where(row == n_row - 1, 0, row + 1), row), jnp.where(wrap_up, 0, col + 1))
    down = (jnp.where(wrap_down, jnp.where(row == 0, n_row - 1, row - 1), row), jnp.where(wrap_down, n_col - 1, col - 1))
    here = (row, col)
    far = 4 - base

    def pick(cond, x, y):
        return tuple(jnp.where(cond, p, q) for p, q in zip(x, y))

    peer = {
        1: pick(b == 0, (*here, base + 3), (*up, far + 1)),
        -1: pick(b == 0, (*down, far + 3), (*here, base + 1)),
    }
    slot_up = jnp.where(first, 0, 1)
    slot_up_before = jnp.where((row == 0) & (col == 1), 0, 1)
    slot_down = jnp.where(first, 1, 0)
    slot_down_after = jnp.where(last, 1, 0)

    def turn(x, p, n):
        return jnp.where(x + p >= n, x + p - n, x + p)

    def remote(src, dst, send, recv, to):
        return pltpu.make_async_remote_copy(src, dst, send, recv, device_id=to, device_id_type=MESH)

    def arrived(ref, sem):
        pltpu.make_async_copy(ref, ref, sem).wait()

    others = [(row, col, turn(layer, p, n_layer)) for p in range(1, n_layer)]
    adder = layer == 0
    col_peers = [(row, turn(col, p, n_col), layer) for p in range(1, n_col)]
    row_peers = [(turn(row, p, n_row), col, layer) for p in range(1, n_row)]

    barrier = pltpu.get_barrier_semaphore()

    def greet(to):
        pl.semaphore_signal(barrier, inc=1, device_id=to, device_id_type=MESH)

    def ready(group, start, columns):
        for k in columns:
            greet((*group, turn(start, k, n_layer)))

    @pl.when(u == 1)
    def _():
        ready(here, base, (0, 2, 3))
        ready(down, far, (2, 3, 4, 5, 6, 7))
        ready(up, far, (4, 5, 6, 7))

    @pl.when(u == 3)
    def _():
        ready(here, base, (0, 1, 2, 4, 5))
        ready(down, far, (6, 7))
        ready(up, far, (0, 1, 6, 7))

    for k in range(2):
        @pl.when(u != 1 + 2 * k)
        def _():
            greet((*here, base + 1 + 2 * k))

    greet((*down, far + 3))
    greet((*up, far + 1))

    @pl.when(jnp.logical_not(adder))
    def _():
        greet((*here, 0))

    def sources(a):
        pair, d, q = a // 2, u - a, u - 2 * (a // 2)
        two, four = jnp.where(q >= 2, 1, 0), jnp.where(q >= 4, 1, 0)
        n = q + 1 + 2 * two + four if a % 2 else q + two + 2 * four
        has = (d >= 0) & (d <= ROWS)
        block = blk_ref.at[a, jnp.where(d == ROWS, slot_up, 0)]
        mine_, next_ = (*here, base + 1 + 2 * pair), ((*here, base + 3) if a < 2 else (*up, far + 1))
        third = (*up, far + 1) if a < 2 else (*up, far + 3)
        yield has & (q < 2), block, right.at[0, n], grecv.at[2, n], (*down, far + 3) if a < 2 else (*here, base + 1), False
        yield has, block, left.at[0, n], grecv.at[1, n], pick(q >= 4, third, next_), u == 3 if a < 2 else False
        yield has, block, own.at[0, n], grecv.at[0, n], pick(q >= 4, next_, mine_), u == 1 + 2 * pair
        c = jnp.where(u < ROWS, u, u - n_layer) - 2 * pair + 2
        n = jnp.where(c >= 0, 3 + a % 2 + 2 * c, 9 + a % 2 + c)
        has = (u >= a + ROWS) | (u < 2) if a >= 2 else u >= a + ROWS
        block = blk_ref.at[a, jnp.where(u == a + ROWS, slot_down, 0)]
        yield has, block, right.at[0, n], grecv.at[2, n], (*down, far + 1 + 2 * pair), False

    plans = list(zip(*(sources(a) for a in range(ROWS))))
    @pl.when(collector)
    def _():
        for to in peer.values():
            greet(to)
        pl.semaphore_wait(barrier, 2 + (n_layer - 1) + n_layer + 2)

    @pl.when(adder)
    def _():
        for to in [*col_peers, *row_peers]:
            greet(to)
        pl.semaphore_wait(barrier, 3 + (n_layer - 1) + (n_col - 1) + (n_row - 1))

    @pl.when(jnp.logical_not(collector | adder) & (u < 6))
    def _():
        pl.semaphore_wait(barrier, 3)

    @pl.when(u >= 6)
    def _():
        pl.semaphore_wait(barrier, 4)

    for k, plan in enumerate(plans):
        for a, (has, block, dst, sem, to, local) in enumerate(plan):
            @pl.when(has & jnp.logical_not(local))
            def _():
                remote(block, dst, gsend.at[k, a], sem, to).start()

            if local is not False:
                @pl.when(has & local)
                def _():
                    pltpu.make_async_copy(block, dst, sem).start()

    zero[...] = jnp.zeros_like(zero)
    for a in range(ROWS):
        @pl.when(u != a + ROWS)
        def _():
            pltpu.make_async_copy(zero, out_ref.at[a, 1], zsem.at[a]).start()

    def copy(tile, way, t):
        part = pl.ds(*SPAN[tile])
        k = 2 * list(SPAN).index(tile) + (way == UP)
        dst = left if way == UP else right
        return remote(own.at[t, part], dst.at[t, part], hsend.at[t, k], hrecv.at[t, k], peer[way])

    def come(tile, way, t):
        part = pl.ds(*SPAN[tile])
        k = 2 * list(SPAN).index(tile) + (way == UP)
        dst = left if way == UP else right
        blocks = range(SPAN[tile][0], sum(SPAN[tile]))
        turned = way == DOWN and tile != "A"

        @pl.when(t == 0)
        def _():
            for n in blocks:
                arrived(dst.at[0, n], grecv.at[1 if way == UP else 2, n])
            if turned:
                for n in blocks:
                    a, q = BLOCKS[n]
                    put(a + 2, q + 2, dst[0, n].T)

        @pl.when(t > 0)
        def _():
            arrived(dst.at[t, part], hrecv.at[t, k])
            if turned:
                for n in blocks:
                    a, q = BLOCKS[n]
                    put(a + 2, q + 2, dst[t, n])

        if not turned:
            for n in blocks:
                a, q = BLOCKS[n]
                put_both(a - 2 * way, q - 2 * way, dst[t, n])

    def put(r, k, x):
        h = x.astype(jnp.bfloat16)
        at = ((r + 2) // 2 * 4 + r % 2) * B
        split[at:at + B, (k + 4) * B:(k + 5) * B] = h
        split[at + 2 * B:at + 3 * B, (k + 4) * B:(k + 5) * B] = (x - h.astype(jnp.float32)).astype(jnp.bfloat16)

    def put_both(r, k, x):
        if -2 <= r < 4:
            put(r, k, x)
        if k > r and -2 <= k < 4:
            put(k, r, x.T)

    def product(tile, start, stop):
        i, j = CORNER[tile]

        def part(r, first, last):
            at = (r + 2) * 2 * B
            return split[at + first * B:at + last * B, (start + 4) * B:(stop + 4) * B]

        def dot(x, y):
            return lax.dot_general(x, y, (((1,), (1,)), ((), ())), preferred_element_type=jnp.float32)

        both = dot(part(i, 0, 4), part(j, 0, 2))
        if tile == "A":
            return both
        return both[:2 * B] + (both[2 * B:] + dot(part(i, 0, 2), part(j, 2, 4)))

    def whole(both):
        return both[:2 * B] + (both[2 * B:] + both[2 * B:].T)

    def there(a, q):
        at_row = ROWS * (row * n_col + col) + 2 * b + a
        at_col = at_row + q - a
        slot = 2 * turn(base + 2 * b, q, n_layer)
        r = jnp.maximum(at_row, 0)
        return (at_row >= 0) & ((cols_ref[slot, r] == at_col) | (cols_ref[slot + 1, r] == at_col))

    def finish(t, tile, total, masks):
        square = signs_ref[t] == 1
        keep = jnp.where(square, 0.0, 2.0).astype(jnp.float32)
        sign = jnp.where(square, 1.0, -1.0).astype(jnp.float32)
        start, size = SPAN[tile]
        for n in range(start, start + size):
            a, q = BLOCKS[n]
            factor = sign * masks[n]
            part = total[(a % 2) * B:(a % 2 + 1) * B, (q % 2) * B:(q % 2 + 1) * B]
            own[t + 1, n] = keep * own[t, n] + factor * part

    def results(tile):
        start, size = SPAN[tile]
        for n in range(start, start + size):
            a, q = BLOCKS[n]
            wide = q - a == ROWS
            at_a, at_q = turn(base + 2 * b, a % n_layer, n_layer), turn(base + 2 * b, q, n_layer)
            if a >= 0:
                group, r, slot = here, 2 * b + a, 0
            else:
                group = pick(b == 0, down, here)
                r = jnp.where(b == 0, ROWS + a, 2 + a)
                slot = jnp.where(b == 0, slot_up_before, slot_up) if wide else 0
            yield own.at[STEPS, n], out_ref.at[r, slot], osend.at[0, n], orecv.at[r, slot], (*group, at_q), q == 1
            if q > a:
                over = 2 * b + q >= ROWS
                group = pick(over, up, here)
                r = jnp.where(over, 2 * b + q - ROWS, 2 * b + q)
                slot = jnp.where(over, slot_down_after, slot_down) if wide else 0
                local = b == 0 if a == 1 else False
                yield flip.at[n], out_ref.at[r, slot], osend.at[1, n], orecv.at[r, slot], (*group, at_a), local

    def deliver(tile):
        start, size = SPAN[tile]
        for n in range(start, start + size):
            a, q = BLOCKS[n]
            if q > a:
                flip[n] = own[STEPS, n].T
        for src, dst, send, recv, to, local in results(tile):
            if local is not True:
                @pl.when(jnp.logical_not(local))
                def _():
                    remote(src, dst, send, recv, to).start()
            if local is not False:
                @pl.when(local)
                def _():
                    pltpu.make_async_copy(src, dst, recv).start()

    def delivered(tile):
        for src, dst, send, recv, to, local in results(tile):
            if local is not True:
                @pl.when(jnp.logical_not(local))
                def _():
                    remote(src, dst, send, recv, to).wait_send()

    def share():
        eye = lax.broadcasted_iota(i32, (B, B), 0) == lax.broadcasted_iota(i32, (B, B), 1)

        def diagonal(t):
            return jnp.sum(jnp.where(eye, own[t, 0] + own[t, 2], 0.0), axis=0, keepdims=True)

        one, two = diagonal(1), diagonal(2)
        diag = jnp.zeros((B, B), jnp.float32)
        off = jnp.zeros((B, B), jnp.float32)
        for n, (a, q) in enumerate(BLOCKS):
            x = own[2, n]
            if q > a:
                off = off + x * x
            else:
                diag = diag + x * x
        norm = jnp.sum(diag + 2.0 * off, axis=0, keepdims=True)
        three = jnp.where(signs_ref[2] == 1, norm, 2.0 * two - norm)
        line = lax.broadcasted_iota(i32, (8, B), 0)
        mine[...] = jnp.where(line == 0, one, jnp.where(line == 1, two, jnp.where(line == 2, three, 0.0)))
        remote(mine, tb0.at[b], t0s, t0r.at[b], (*here, 0)).start()

    @pl.when(adder)
    def _():
        for k in range(2):
            arrived(tb0.at[k], t0r.at[k])
        tb1[col] = tb0[0] + tb0[1]
        for p, to in enumerate(col_peers):
            remote(tb1.at[col], tb1.at[col], t1s.at[p], t1r.at[col], to).start()
        for p in range(1, n_col):
            c = turn(col, p, n_col)
            arrived(tb1.at[c], t1r.at[c])
        tb2[row] = jnp.sum(tb1[...], axis=0)
        for p, to in enumerate(row_peers):
            remote(tb2.at[row], tb2.at[row], t2s.at[p], t2r.at[row], to).start()
        for p in range(1, n_row):
            r = turn(row, p, n_row)
            arrived(tb2.at[r], t2r.at[r])
        total = jnp.sum(jnp.sum(tb2[...], axis=0), axis=1, keepdims=True) / (n_row * n_col * ROWS * B)
        mine[...] = jnp.broadcast_to(total, (8, B))
        for p, to in enumerate(others):
            remote(mine, tb3, t3s.at[p], t3r, to).start()
        tb3[...] = mine[...]
        for p, to in enumerate(col_peers):
            remote(tb1.at[col], tb1.at[col], t1s.at[p], t1r.at[col], to).wait_send()
        for p, to in enumerate(row_peers):
            remote(tb2.at[row], tb2.at[row], t2s.at[p], t2r.at[row], to).wait_send()
        for p, to in enumerate(others):
            remote(mine, tb3, t3s.at[p], t3r, to).wait_send()

    @pl.when(collector)
    def _():
        for r, k in ((0, 5), (1, -4), (3, -2), (-2, 3)):
            put(r, k, jnp.zeros((B, B), jnp.float32))
        masks = [jnp.where(there(a, q), 1.0, 0.0).astype(jnp.float32) for a, q in BLOCKS]

        for n in range(len(BLOCKS)):
            arrived(own.at[0, n], grecv.at[0, n])

        def step(t, carry):
            pl.when(t == 2)(share)
            for n, (a, q) in enumerate(BLOCKS):
                put_both(a, q, own[t, n])
            def within():
                acc_a[...] = product("A", 0, 4)
                acc_b[...] = product("B", 0, 2)

            pl.when(t > 0)(within)

            def send(when, *copies):
                @pl.when(when)
                def _():
                    for tile, way in copies:
                        copy(tile, way, t + 1).start()

            def make_d(even):
                come("A", DOWN, t)
                come("A", UP, t)
                finish(t, "D", product("D", -2, 4), masks)
                if even:
                    send(t == 0, ("D", UP), ("D", DOWN))
                    pl.when(t == 2)(lambda: deliver("D"))
                else:
                    copy("D", DOWN, 2).start()

            come("B", UP, t)
            pl.when(t != 1)(lambda: make_d(True))
            pl.when(t == 0)(within)
            def make_a():
                finish(t, "A", whole(acc_a[...] + product("A", -4, 0) + product("A", 4, 6)), masks)

            def make_b():
                come("B", DOWN, t)
                finish(t, "B", acc_b[...] + product("B", -2, 0) + product("B", 2, 6), masks)

            come("D", DOWN, t)

            @pl.when(t < 2)
            def _():
                come("D", UP, t)
                make_a()
                copy("A", DOWN, t + 1).start()
                send(t == 1, ("A", UP))
                pl.when(t == 1)(lambda: make_d(False))
                make_b()
                copy("B", UP, t + 1).start()
                copy("B", DOWN, t + 1).start()
                send(t == 0, ("A", UP))
                send(t == 1, ("D", UP))

            @pl.when(t == 2)
            def _():
                make_b()
                deliver("B")
                come("D", UP, t)
                make_a()
                deliver("A")

            return carry

        lax.fori_loop(0, STEPS, step, 0)

        for t in range(1, STEPS):
            for tile in SPAN:
                for way in (UP, DOWN):
                    copy(tile, way, t).wait_send()
        for tile in SPAN:
            delivered(tile)

        remote(mine, tb0.at[b], t0s, t0r.at[b], (*here, 0)).wait_send()

    for k, plan in enumerate(plans):
        for a, (has, block, dst, sem, to, local) in enumerate(plan):
            @pl.when(has & jnp.logical_not(local))
            def _():
                remote(block, dst, gsend.at[k, a], sem, to).wait_send()

    @pl.when(jnp.logical_not(adder))
    def _():
        arrived(tb3, t3r)

    for t in range(STEPS):
        tr_ref[t] = tb3[t, 0]
    for a in range(ROWS):
        arrived(out_ref.at[a, 0], orecv.at[a, 0])

        @pl.when(u == a + ROWS)
        def _():
            arrived(out_ref.at[a, 1], orecv.at[a, 1])

        @pl.when(u != a + ROWS)
        def _():
            pltpu.make_async_copy(zero, out_ref.at[a, 1], zsem.at[a]).wait()


def hand_over(out_ref, tr_ref, result_ref, traces_ref):
    result_ref[...] = out_ref[...]
    for t in range(STEPS):
        traces_ref[t] = tr_ref[t]


def solution(mesh):
    n_row, n_col, n_layer = (mesh.shape[name] for name in ("row", "col", "layer"))
    dma = pltpu.SemaphoreType.DMA

    def shards(blocks, columns, signs):
        def body(*refs):
            kernel(n_row, n_col, n_layer, *refs)

        f32, bf16 = jnp.float32, jnp.bfloat16
        out, traces = pl.pallas_call(
            body,
            out_shape=(jax.ShapeDtypeStruct(blocks.shape, f32), jax.ShapeDtypeStruct((STEPS,), f32)),
            in_specs=[
                pl.BlockSpec(memory_space=pltpu.SMEM),
                pl.BlockSpec(memory_space=pltpu.SMEM),
                pl.BlockSpec(memory_space=pltpu.HBM),
            ],
            out_specs=(pl.BlockSpec(memory_space=pl.ANY), pl.BlockSpec(memory_space=pltpu.SMEM)),
            scratch_shapes=[
                pltpu.VMEM((STEPS + 1, 10, B, B), f32),
                pltpu.VMEM((STEPS, 10, B, B), f32),
                pltpu.VMEM((STEPS, 10, B, B), f32),
                pltpu.VMEM((12 * B, 10 * B), bf16),
                pltpu.VMEM((4 * B, 2 * B), f32),
                pltpu.VMEM((2 * B, 2 * B), f32),
                pltpu.VMEM((10, B, B), f32),
                pltpu.VMEM((B, B), f32),
                pltpu.VMEM((8, B), f32),
                pltpu.VMEM((2, 8, B), f32),
                pltpu.VMEM((n_col, 8, B), f32),
                pltpu.VMEM((n_row, 8, B), f32),
                pltpu.VMEM((8, B), f32),
                dma((4, ROWS)),
                dma((3, 10)),
                dma((STEPS, 6)),
                dma((STEPS, 6)),
                dma((2, 10)),
                dma((ROWS, 2)),
                dma((ROWS,)),
                dma,
                dma((2,)),
                dma((n_col,)),
                dma((n_col,)),
                dma((n_row,)),
                dma((n_row,)),
                dma((n_layer,)),
                dma,
            ],
            compiler_params=pltpu.CompilerParams(
                collective_id=0, has_side_effects=True, vmem_limit_bytes=60 * 1024 * 1024
            ),
        )(columns.T, signs, blocks)
        half = pl.BlockSpec((ROWS // 2, 2, B, B), lambda i: (i, 0, 0, 0))
        return pl.pallas_call(
            hand_over,
            grid=(2,),
            out_shape=(jax.ShapeDtypeStruct(blocks.shape, f32), jax.ShapeDtypeStruct((STEPS,), f32)),
            in_specs=[half, pl.BlockSpec(memory_space=pltpu.SMEM)],
            out_specs=(half, pl.BlockSpec(memory_space=pltpu.SMEM)),
            compiler_params=pltpu.CompilerParams(vmem_limit_bytes=60 * 1024 * 1024),
        )(out, traces)

    return jax.shard_map(
        shards,
        mesh=mesh,
        in_specs=(P(("row", "col"), "layer", None, None), P(), P()),
        out_specs=(P(("row", "col"), "layer", None, None), P()),
        check_vma=False,
    )
```

```python
import jax
import jax.numpy as jnp
from jax import lax
from jax.experimental import pallas as pl
from jax.experimental.pallas import tpu as pltpu
from jax.sharding import PartitionSpec as P

MESH = pl.DeviceIdType.MESH
B = 128
ROWS = 4
STEPS = 3
BLOCKS = ((0, 0), (0, 1), (1, 1), (0, 2), (0, 3), (1, 2), (1, 3), (-2, 2), (-1, 2), (-1, 3))
SPAN = {"A": (0, 3), "B": (3, 4), "D": (7, 3)}
CORNER = {"A": (0, 0), "B": (0, 2), "D": (-2, 2)}
UP, DOWN = 1, -1


def kernel(n_row, n_col, n_layer, cols_ref, signs_ref, blk_ref, out_ref, tr_ref, own, left, right, split, acc_a, acc_b,
           flip, zero, mine, tb0, tb1, tb2, tb3, gsend, grecv, hsend, hrecv, osend, orecv, zsem, t0s, t0r, t1s, t1r, t2s, t2r,
           t3s, t3r):
    row, col, layer = lax.axis_index("row"), lax.axis_index("col"), lax.axis_index("layer")
    i32 = jnp.int32
    core = lax.rem(col, 2)
    base = 4 * core
    u = jnp.where(layer < base, layer - base + n_layer, layer - base)
    collector = (u == 1) | (u == 3)
    b = jnp.where(u == 3, 1, 0)
    first = (row == 0) & (col == 0)
    last = (row == n_row - 1) & (col == n_col - 1)
    wrap_up, wrap_down = col == n_col - 1, col == 0
    up = (jnp.where(wrap_up, jnp.where(row == n_row - 1, 0, row + 1), row), jnp.where(wrap_up, 0, col + 1))
    down = (jnp.where(wrap_down, jnp.where(row == 0, n_row - 1, row - 1), row), jnp.where(wrap_down, n_col - 1, col - 1))
    here = (row, col)
    far = 4 - base

    def pick(cond, x, y):
        return tuple(jnp.where(cond, p, q) for p, q in zip(x, y))

    peer = {
        1: pick(b == 0, (*here, base + 3), (*up, far + 1)),
        -1: pick(b == 0, (*down, far + 3), (*here, base + 1)),
    }
    slot_up = jnp.where(first, 0, 1)
    slot_up_before = jnp.where((row == 0) & (col == 1), 0, 1)
    slot_down = jnp.where(first, 1, 0)
    slot_down_after = jnp.where(last, 1, 0)

    def turn(x, p, n):
        return jnp.where(x + p >= n, x + p - n, x + p)

    def remote(src, dst, send, recv, to):
        return pltpu.make_async_remote_copy(src, dst, send, recv, device_id=to, device_id_type=MESH)

    def arrived(ref, sem):
        pltpu.make_async_copy(ref, ref, sem).wait()

    others = [(row, col, turn(layer, p, n_layer)) for p in range(1, n_layer)]
    adder = layer == 0
    col_peers = [(row, turn(col, p, n_col), layer) for p in range(1, n_col)]
    row_peers = [(turn(row, p, n_row), col, layer) for p in range(1, n_row)]

    barrier = pltpu.get_barrier_semaphore()

    def greet(to):
        pl.semaphore_signal(barrier, inc=1, device_id=to, device_id_type=MESH)

    def ready(group, start, columns):
        for k in columns:
            greet((*group, turn(start, k, n_layer)))

    @pl.when(u == 1)
    def _():
        ready(here, base, (0, 2, 3))
        ready(down, far, (2, 3, 4, 5, 6, 7))
        ready(up, far, (4, 5, 6, 7))

    @pl.when(u == 3)
    def _():
        ready(here, base, (0, 1, 2, 4, 5))
        ready(down, far, (6, 7))
        ready(up, far, (0, 1, 6, 7))

    for k in range(2):
        @pl.when(u != 1 + 2 * k)
        def _():
            greet((*here, base + 1 + 2 * k))

    greet((*down, far + 3))
    greet((*up, far + 1))

    @pl.when(jnp.logical_not(adder))
    def _():
        greet((*here, 0))

    def sources(a):
        pair, d, q = a // 2, u - a, u - 2 * (a // 2)
        two, four = jnp.where(q >= 2, 1, 0), jnp.where(q >= 4, 1, 0)
        n = q + 1 + 2 * two + four if a % 2 else q + two + 2 * four
        has = (d >= 0) & (d <= ROWS)
        block = blk_ref.at[a, jnp.where(d == ROWS, slot_up, 0)]
        mine_, next_ = (*here, base + 1 + 2 * pair), ((*here, base + 3) if a < 2 else (*up, far + 1))
        third = (*up, far + 1) if a < 2 else (*up, far + 3)
        yield has & (q < 2), block, right.at[0, n], grecv.at[2, n], (*down, far + 3) if a < 2 else (*here, base + 1), False
        yield has, block, left.at[0, n], grecv.at[1, n], pick(q >= 4, third, next_), u == 3 if a < 2 else False
        yield has, block, own.at[0, n], grecv.at[0, n], pick(q >= 4, next_, mine_), u == 1 + 2 * pair
        c = jnp.where(u < ROWS, u, u - n_layer) - 2 * pair + 2
        n = jnp.where(c >= 0, 3 + a % 2 + 2 * c, 9 + a % 2 + c)
        has = (u >= a + ROWS) | (u < 2) if a >= 2 else u >= a + ROWS
        block = blk_ref.at[a, jnp.where(u == a + ROWS, slot_down, 0)]
        yield has, block, right.at[0, n], grecv.at[2, n], (*down, far + 1 + 2 * pair), False

    plans = list(zip(*(sources(a) for a in range(ROWS))))
    @pl.when(collector)
    def _():
        for to in peer.values():
            greet(to)
        pl.semaphore_wait(barrier, 2 + (n_layer - 1) + n_layer + 2)

    @pl.when(adder)
    def _():
        for to in [*col_peers, *row_peers]:
            greet(to)
        pl.semaphore_wait(barrier, 3 + (n_layer - 1) + (n_col - 1) + (n_row - 1))

    @pl.when(jnp.logical_not(collector | adder) & (u < 6))
    def _():
        pl.semaphore_wait(barrier, 3)

    @pl.when(u >= 6)
    def _():
        pl.semaphore_wait(barrier, 4)

    for k, plan in enumerate(plans):
        for a, (has, block, dst, sem, to, local) in enumerate(plan):
            @pl.when(has & jnp.logical_not(local))
            def _():
                remote(block, dst, gsend.at[k, a], sem, to).start()

            if local is not False:
                @pl.when(has & local)
                def _():
                    pltpu.make_async_copy(block, dst, sem).start()

    zero[...] = jnp.zeros_like(zero)
    for a in range(ROWS):
        @pl.when(u != a + ROWS)
        def _():
            pltpu.make_async_copy(zero, out_ref.at[a, 1], zsem.at[a]).start()

    def copy(tile, way, t):
        part = pl.ds(*SPAN[tile])
        k = 2 * list(SPAN).index(tile) + (way == UP)
        dst = left if way == UP else right
        return remote(own.at[t, part], dst.at[t, part], hsend.at[t, k], hrecv.at[t, k], peer[way])

    def come(tile, way, t):
        part = pl.ds(*SPAN[tile])
        k = 2 * list(SPAN).index(tile) + (way == UP)
        dst = left if way == UP else right
        blocks = range(SPAN[tile][0], sum(SPAN[tile]))
        turned = way == DOWN and tile != "A"

        @pl.when(t == 0)
        def _():
            for n in blocks:
                arrived(dst.at[0, n], grecv.at[1 if way == UP else 2, n])
            if turned:
                for n in blocks:
                    a, q = BLOCKS[n]
                    put(a + 2, q + 2, dst[0, n].T)

        @pl.when(t > 0)
        def _():
            arrived(dst.at[t, part], hrecv.at[t, k])
            if turned:
                for n in blocks:
                    a, q = BLOCKS[n]
                    put(a + 2, q + 2, dst[t, n])

        if not turned:
            for n in blocks:
                a, q = BLOCKS[n]
                put_both(a - 2 * way, q - 2 * way, dst[t, n])

    def put(r, k, x):
        h = x.astype(jnp.bfloat16)
        at = ((r + 2) // 2 * 4 + r % 2) * B
        split[at:at + B, (k + 4) * B:(k + 5) * B] = h
        split[at + 2 * B:at + 3 * B, (k + 4) * B:(k + 5) * B] = (x - h.astype(jnp.float32)).astype(jnp.bfloat16)

    def put_both(r, k, x):
        if -2 <= r < 4:
            put(r, k, x)
        if k > r and -2 <= k < 4:
            put(k, r, x.T)

    def product(tile, start, stop):
        i, j = CORNER[tile]

        def part(r, first, last):
            at = (r + 2) * 2 * B
            return split[at + first * B:at + last * B, (start + 4) * B:(stop + 4) * B]

        def dot(x, y):
            return lax.dot_general(x, y, (((1,), (1,)), ((), ())), preferred_element_type=jnp.float32)

        both = dot(part(i, 0, 4), part(j, 0, 2))
        if tile == "A":
            return both
        return both[:2 * B] + (both[2 * B:] + dot(part(i, 0, 2), part(j, 2, 4)))

    def whole(both):
        return both[:2 * B] + (both[2 * B:] + both[2 * B:].T)

    def there(a, q):
        at_row = ROWS * (row * n_col + col) + 2 * b + a
        at_col = at_row + q - a
        slot = 2 * turn(base + 2 * b, q, n_layer)
        r = jnp.maximum(at_row, 0)
        return (at_row >= 0) & ((cols_ref[slot, r] == at_col) | (cols_ref[slot + 1, r] == at_col))

    def finish(t, tile, total, masks):
        square = signs_ref[t] == 1
        keep = jnp.where(square, 0.0, 2.0).astype(jnp.float32)
        sign = jnp.where(square, 1.0, -1.0).astype(jnp.float32)
        start, size = SPAN[tile]
        for n in range(start, start + size):
            a, q = BLOCKS[n]
            factor = sign * masks[n]
            part = total[(a % 2) * B:(a % 2 + 1) * B, (q % 2) * B:(q % 2 + 1) * B]
            own[t + 1, n] = keep * own[t, n] + factor * part

    def results(tile):
        start, size = SPAN[tile]
        for n in range(start, start + size):
            a, q = BLOCKS[n]
            wide = q - a == ROWS
            at_a, at_q = turn(base + 2 * b, a % n_layer, n_layer), turn(base + 2 * b, q, n_layer)
            if a >= 0:
                group, r, slot = here, 2 * b + a, 0
            else:
                group = pick(b == 0, down, here)
                r = jnp.where(b == 0, ROWS + a, 2 + a)
                slot = jnp.where(b == 0, slot_up_before, slot_up) if wide else 0
            yield None, (own.at[STEPS, n], out_ref.at[r, slot], osend.at[0, n], orecv.at[r, slot], (*group, at_q), q == 1)
            if q > a:
                over = 2 * b + q >= ROWS
                group = pick(over, up, here)
                r = jnp.where(over, 2 * b + q - ROWS, 2 * b + q)
                slot = jnp.where(over, slot_down_after, slot_down) if wide else 0
                local = b == 0 if a == 1 else False
                yield n, (flip.at[n], out_ref.at[r, slot], osend.at[1, n], orecv.at[r, slot], (*group, at_a), local)

    def deliver(tile):
        def start(src, dst, send, recv, to, local):
            if local is not True:
                @pl.when(jnp.logical_not(local))
                def _():
                    remote(src, dst, send, recv, to).start()
            if local is not False:
                @pl.when(local)
                def _():
                    pltpu.make_async_copy(src, dst, recv).start()

        plan = list(results(tile))
        for turned, result in plan:
            if turned is None:
                start(*result)
        for turned, result in plan:
            if turned is not None:
                flip[turned] = own[STEPS, turned].T
                start(*result)

    def delivered(tile):
        for _, (src, dst, send, recv, to, local) in results(tile):
            if local is not True:
                @pl.when(jnp.logical_not(local))
                def _():
                    remote(src, dst, send, recv, to).wait_send()

    def share():
        eye = lax.broadcasted_iota(i32, (B, B), 0) == lax.broadcasted_iota(i32, (B, B), 1)

        def diagonal(t):
            return jnp.sum(jnp.where(eye, own[t, 0] + own[t, 2], 0.0), axis=0, keepdims=True)

        one, two = diagonal(1), diagonal(2)
        diag = jnp.zeros((B, B), jnp.float32)
        off = jnp.zeros((B, B), jnp.float32)
        for n, (a, q) in enumerate(BLOCKS):
            x = own[2, n]
            if q > a:
                off = off + x * x
            else:
                diag = diag + x * x
        norm = jnp.sum(diag + 2.0 * off, axis=0, keepdims=True)
        three = jnp.where(signs_ref[2] == 1, norm, 2.0 * two - norm)
        line = lax.broadcasted_iota(i32, (8, B), 0)
        mine[...] = jnp.where(line == 0, one, jnp.where(line == 1, two, jnp.where(line == 2, three, 0.0)))
        remote(mine, tb0.at[b], t0s, t0r.at[b], (*here, 0)).start()

    @pl.when(adder)
    def _():
        for k in range(2):
            arrived(tb0.at[k], t0r.at[k])
        tb1[col] = tb0[0] + tb0[1]
        for p, to in enumerate(col_peers):
            remote(tb1.at[col], tb1.at[col], t1s.at[p], t1r.at[col], to).start()
        for p in range(1, n_col):
            c = turn(col, p, n_col)
            arrived(tb1.at[c], t1r.at[c])
        tb2[row] = jnp.sum(tb1[...], axis=0)
        for p, to in enumerate(row_peers):
            remote(tb2.at[row], tb2.at[row], t2s.at[p], t2r.at[row], to).start()
        for p in range(1, n_row):
            r = turn(row, p, n_row)
            arrived(tb2.at[r], t2r.at[r])
        total = jnp.sum(jnp.sum(tb2[...], axis=0), axis=1, keepdims=True) / (n_row * n_col * ROWS * B)
        mine[...] = jnp.broadcast_to(total, (8, B))
        for p, to in enumerate(others):
            remote(mine, tb3, t3s.at[p], t3r, to).start()
        tb3[...] = mine[...]
        for p, to in enumerate(col_peers):
            remote(tb1.at[col], tb1.at[col], t1s.at[p], t1r.at[col], to).wait_send()
        for p, to in enumerate(row_peers):
            remote(tb2.at[row], tb2.at[row], t2s.at[p], t2r.at[row], to).wait_send()
        for p, to in enumerate(others):
            remote(mine, tb3, t3s.at[p], t3r, to).wait_send()

    @pl.when(collector)
    def _():
        for r, k in ((0, 5), (1, -4), (3, -2), (-2, 3)):
            put(r, k, jnp.zeros((B, B), jnp.float32))
        masks = [jnp.where(there(a, q), 1.0, 0.0).astype(jnp.float32) for a, q in BLOCKS]

        for n in range(len(BLOCKS)):
            arrived(own.at[0, n], grecv.at[0, n])

        def step(t, carry):
            pl.when(t == 2)(share)
            for n, (a, q) in enumerate(BLOCKS):
                put_both(a, q, own[t, n])
            def within():
                acc_a[...] = product("A", 0, 4)
                acc_b[...] = product("B", 0, 2)

            pl.when(t > 0)(within)

            def send(when, *copies):
                @pl.when(when)
                def _():
                    for tile, way in copies:
                        copy(tile, way, t + 1).start()

            def make_d(even):
                come("A", DOWN, t)
                come("A", UP, t)
                finish(t, "D", product("D", -2, 4), masks)
                if even:
                    send(t == 0, ("D", UP), ("D", DOWN))
                    pl.when(t == 2)(lambda: deliver("D"))
                else:
                    copy("D", DOWN, 2).start()

            come("B", UP, t)
            pl.when(t != 1)(lambda: make_d(True))
            pl.when(t == 0)(within)
            def make_a():
                finish(t, "A", whole(acc_a[...] + product("A", -4, 0) + product("A", 4, 6)), masks)

            def make_b():
                come("B", DOWN, t)
                finish(t, "B", acc_b[...] + product("B", -2, 0) + product("B", 2, 6), masks)

            come("D", DOWN, t)

            @pl.when(t < 2)
            def _():
                come("D", UP, t)
                make_a()
                copy("A", DOWN, t + 1).start()
                send(t == 1, ("A", UP))
                pl.when(t == 1)(lambda: make_d(False))
                make_b()
                copy("B", UP, t + 1).start()
                copy("B", DOWN, t + 1).start()
                send(t == 0, ("A", UP))
                send(t == 1, ("D", UP))

            @pl.when(t == 2)
            def _():
                make_b()
                deliver("B")
                come("D", UP, t)
                make_a()
                deliver("A")

            return carry

        lax.fori_loop(0, STEPS, step, 0)

        for t in range(1, STEPS):
            for tile in SPAN:
                for way in (UP, DOWN):
                    copy(tile, way, t).wait_send()
        for tile in SPAN:
            delivered(tile)

        remote(mine, tb0.at[b], t0s, t0r.at[b], (*here, 0)).wait_send()

    for k, plan in enumerate(plans):
        for a, (has, block, dst, sem, to, local) in enumerate(plan):
            @pl.when(has & jnp.logical_not(local))
            def _():
                remote(block, dst, gsend.at[k, a], sem, to).wait_send()

    @pl.when(jnp.logical_not(adder))
    def _():
        arrived(tb3, t3r)

    for t in range(STEPS):
        tr_ref[t] = tb3[t, 0]
    for a in range(ROWS):
        arrived(out_ref.at[a, 0], orecv.at[a, 0])

        @pl.when(u == a + ROWS)
        def _():
            arrived(out_ref.at[a, 1], orecv.at[a, 1])

        @pl.when(u != a + ROWS)
        def _():
            pltpu.make_async_copy(zero, out_ref.at[a, 1], zsem.at[a]).wait()


def hand_over(out_ref, tr_ref, result_ref, traces_ref):
    result_ref[...] = out_ref[...]
    for t in range(STEPS):
        traces_ref[t] = tr_ref[t]


def solution(mesh):
    n_row, n_col, n_layer = (mesh.shape[name] for name in ("row", "col", "layer"))
    dma = pltpu.SemaphoreType.DMA

    def shards(blocks, columns, signs):
        def body(*refs):
            kernel(n_row, n_col, n_layer, *refs)

        f32, bf16 = jnp.float32, jnp.bfloat16
        out, traces = pl.pallas_call(
            body,
            out_shape=(jax.ShapeDtypeStruct(blocks.shape, f32), jax.ShapeDtypeStruct((STEPS,), f32)),
            in_specs=[
                pl.BlockSpec(memory_space=pltpu.SMEM),
                pl.BlockSpec(memory_space=pltpu.SMEM),
                pl.BlockSpec(memory_space=pltpu.HBM),
            ],
            out_specs=(pl.BlockSpec(memory_space=pl.ANY), pl.BlockSpec(memory_space=pltpu.SMEM)),
            scratch_shapes=[
                pltpu.VMEM((STEPS + 1, 10, B, B), f32),
                pltpu.VMEM((STEPS, 10, B, B), f32),
                pltpu.VMEM((STEPS, 10, B, B), f32),
                pltpu.VMEM((12 * B, 10 * B), bf16),
                pltpu.VMEM((4 * B, 2 * B), f32),
                pltpu.VMEM((2 * B, 2 * B), f32),
                pltpu.VMEM((10, B, B), f32),
                pltpu.VMEM((B, B), f32),
                pltpu.VMEM((8, B), f32),
                pltpu.VMEM((2, 8, B), f32),
                pltpu.VMEM((n_col, 8, B), f32),
                pltpu.VMEM((n_row, 8, B), f32),
                pltpu.VMEM((8, B), f32),
                dma((4, ROWS)),
                dma((3, 10)),
                dma((STEPS, 6)),
                dma((STEPS, 6)),
                dma((2, 10)),
                dma((ROWS, 2)),
                dma((ROWS,)),
                dma,
                dma((2,)),
                dma((n_col,)),
                dma((n_col,)),
                dma((n_row,)),
                dma((n_row,)),
                dma((n_layer,)),
                dma,
            ],
            compiler_params=pltpu.CompilerParams(
                collective_id=0, has_side_effects=True, vmem_limit_bytes=60 * 1024 * 1024
            ),
        )(columns.T, signs, blocks)
        half = pl.BlockSpec((ROWS // 2, 2, B, B), lambda i: (i, 0, 0, 0))
        return pl.pallas_call(
            hand_over,
            grid=(2,),
            out_shape=(jax.ShapeDtypeStruct(blocks.shape, f32), jax.ShapeDtypeStruct((STEPS,), f32)),
            in_specs=[half, pl.BlockSpec(memory_space=pltpu.SMEM)],
            out_specs=(half, pl.BlockSpec(memory_space=pltpu.SMEM)),
            compiler_params=pltpu.CompilerParams(vmem_limit_bytes=60 * 1024 * 1024),
        )(out, traces)

    return jax.shard_map(
        shards,
        mesh=mesh,
        in_specs=(P(("row", "col"), "layer", None, None), P(), P()),
        out_specs=(P(("row", "col"), "layer", None, None), P()),
        check_vma=False,
    )
```
